32 devices in a mesh: parts: 1, gx: 4 (over z), gy: 4 (over y, x), gz: 2 (over core).
Axes of the slice: x: 2, y: 2, z: 4, core: 2. Of those that a mesh axis runs over, the one named last changes fastest.
Arguments:
- state_field: bfloat16 [8, 12, 128, 128, 128], P('parts', None, 'gx', ('gy', 'gz')), may hold values from -6 to 6
- cotangent: bfloat16 [8, 12, 128, 128, 128], P('parts', None, 'gx', ('gy', 'gz')), may hold values from -6 to 6
- spectral_weight: bfloat16 [32, 32, 12, 12, 4, 32], P(('gy', 'gz'), 'gx'), may hold values from -12 to 12
- point_weight: bfloat16 [12, 12], replicated, may hold values from -1.75 to 1.75
Outputs:
- grad_field: bfloat16 [8, 12, 128, 128, 128], P('parts', None, 'gx', ('gy', 'gz'))
- grad_spectral: float32 [32, 32, 12, 12, 4, 32], P(('parts', 'gy', 'gz'), 'gx')
The draws below stay inside these ranges and needn't reach their ends.
All inputs are finite; a program needn't handle non-finite values.
Results may differ from the reference program's by a relative error of at most 0.02.
Values may be sent and summed in bfloat16 or wider, within the bound.
No kernel may reach another device: no remote copies, remote signals or barrier semaphores. Data moves between devices by JAX's collectives and lax.ppermute only.
A program may use at most 256 MiB of HBM per device.

```python
import math
import jax
import jax.numpy as jnp
from jax import lax

C = 12
NT = 8
NX = 128
NY = 128
NZ = 128
KS = 32
KT = 4


def block_scale(key, shape, shards, low, largest):
    factor_of, own = 1.0, jax.random.fold_in(key, 6)
    for dim, shards_of in shards:
        draws = jnp.exp(jax.random.uniform(jax.random.fold_in(own, dim), (shards_of,), jnp.float32, low / len(shards), largest / len(shards)))
        factor_of = factor_of * jnp.repeat(draws, shape[dim] // shards_of).reshape([-1 if axis == dim else 1 for axis in range(len(shape))])
    return factor_of


def bell_draw(stream_key, dims, width, most, shards=(), kind=jnp.bfloat16):
    loudness = block_scale(stream_key, dims, shards, -0.22, 0.18) if shards else 1.0
    entries = jax.random.normal(stream_key, dims, jnp.float32) * width * loudness
    return jnp.minimum(jnp.maximum(entries, -most), most).astype(kind)


def setup_inputs(seed: int = 0, part: int = 0) -> dict:
    key_of = jax.random.split(jax.random.key(seed), 5)
    own_keys = jax.random.split(jax.random.fold_in(key_of[4], part), 5)
    state_field = bell_draw(own_keys[0], (NT, C, NX, NY, NZ), 1.0, 6.0, ((2, 4), (3, 8)))
    cotangent = bell_draw(own_keys[1], (NT, C, NX, NY, NZ), 1.0, 6.0, ((2, 4), (3, 8)))
    spectral_weight = bell_draw(key_of[2], (KS, KS, C, C, KT, KS), 2.0, 12.0, ((0, 8), (1, 4)))
    point_weight = bell_draw(key_of[3], (C, C), C ** -0.5, 1.75)
    return {"state_field": state_field, "cotangent": cotangent, "spectral_weight": spectral_weight, "point_weight": point_weight}


highest = lax.Precision.HIGHEST

def build_table(row_count, extent):
    row_index = jnp.arange(row_count, dtype=jnp.int32)[:, None]
    cell_index = jnp.arange(extent, dtype=jnp.int32)[None, :]
    frequency = (row_index + 1) // 2
    phase_turns = (frequency * cell_index % extent).astype(jnp.float32)
    radians = phase_turns * (2.0 * math.pi / extent)
    waveform = jnp.where(row_index % 2 == 0, jnp.cos(radians), jnp.sin(radians))
    row_scale = jnp.where(row_index == 0, math.sqrt(1.0 / extent), math.sqrt(2.0 / extent))
    return (waveform * row_scale).astype(jnp.bfloat16)

def exact_mix(form, left, right):
    return jnp.einsum(form, left.astype(jnp.float32), right.astype(jnp.float32), precision=highest)

def reference(state_field, cotangent, spectral_weight, point_weight):
    time_table = build_table(KT, NT)
    depth_table = build_table(KS, NZ)
    x_table = build_table(KS, NX)
    y_table = build_table(KS, NY)

    def head(values):
        depth_part = exact_mix('tcxyz,qz->tcxyq', values, depth_table)
        return exact_mix('pt,tcxyq->cxypq', time_table, depth_part).astype(jnp.bfloat16)

    def spectrum(head_modes):
        x_part = exact_mix('ix,cxypq->cyqpi', x_table, head_modes)
        return exact_mix('jy,cyqpi->jcqpi', y_table, x_part).astype(jnp.bfloat16)

    def synthesize(spec_modes):
        y_part = exact_mix('jy,joqpi->oyqpi', y_table, spec_modes)
        return exact_mix('ix,oyqpi->oxypq', x_table, y_part).astype(jnp.bfloat16)

    def tail(middle):
        depth_syn = exact_mix('oxypq,qz->oxypz', middle, depth_table)
        return exact_mix('pt,oxypz->toxyz', time_table, depth_syn)
    modes_in = spectrum(head(state_field))
    modes_out = exact_mix('jcqpi,jqcopi->joqpi', modes_in, spectral_weight).astype(jnp.bfloat16)
    preact = tail(synthesize(modes_out)) + exact_mix('tcxyz,co->toxyz', state_field, point_weight)
    gelu_slope = 0.5 * (1.0 + lax.erf(preact * (1.0 / math.sqrt(2.0)))) + preact * jnp.exp(-0.5 * preact * preact) * (1.0 / math.sqrt(2.0 * math.pi))
    grad_pre = (cotangent.astype(jnp.float32) * gelu_slope).astype(jnp.bfloat16)
    grad_modes = spectrum(head(grad_pre))
    grad_spectral = exact_mix('jcqpi,joqpi->jqcopi', modes_in, grad_modes)
    back_modes = exact_mix('joqpi,jqcopi->jcqpi', grad_modes, spectral_weight).astype(jnp.bfloat16)
    grad_field = tail(synthesize(back_modes)) + exact_mix('toxyz,co->tcxyz', grad_pre, point_weight)
    return (grad_field.astype(jnp.bfloat16), grad_spectral)
```

```python
import functools
import math

import jax
import jax.numpy as jnp
import ml_dtypes
import numpy as np
from jax import lax
from jax.experimental import pallas as pl
from jax.experimental.pallas import tpu as pltpu
from jax.sharding import PartitionSpec as P

YZ = ("gy", "gz")
HALF_ROOT = 1.0 / math.sqrt(2.0)
DENSITY = 1.0 / math.sqrt(2.0 * math.pi)


def basis(row_count, extent):
    row = np.arange(row_count)[:, None]
    cell = np.arange(extent)[None, :]
    radians = ((row + 1) // 2 * cell % extent) * (2.0 * math.pi / extent)
    wave = np.where(row % 2 == 0, np.cos(radians), np.sin(radians))
    scale = np.where(row == 0, math.sqrt(1.0 / extent), math.sqrt(2.0 / extent))
    return (wave * scale).astype(ml_dtypes.bfloat16).astype(np.float32)


def narrow(table):
    return np.asarray(table, dtype=ml_dtypes.bfloat16)


def dot(left, right, left_dim=1, right_dim=0):
    return lax.dot_general(
        left, right, (((left_dim,), (right_dim,)), ((), ())), preferred_element_type=jnp.float32
    )


def gelu_slope(value):
    size = jnp.abs(value)
    bell = jnp.exp(value * value * -0.5)
    t = 1.0 / (1.0 + (0.3275911 * HALF_ROOT) * size)
    tail = t * (
        0.5 * 0.254829592
        + t * (0.5 * -0.284496736 + t * (0.5 * 1.421413741 + t * (0.5 * -1.453152027 + t * (0.5 * 1.061405429))))
    )
    low = bell * (tail - DENSITY * size)
    return jnp.where(value >= 0.0, 1.0 - low, low)


def call(body, grid, in_specs, out_specs, out_shape, flops, moved, args):
    return pl.pallas_call(
        body,
        grid=grid,
        in_specs=in_specs,
        out_specs=out_specs,
        out_shape=out_shape,
        compiler_params=pltpu.CompilerParams(vmem_limit_bytes=48 * 1024 * 1024),
        cost_estimate=pl.CostEstimate(flops=flops, bytes_accessed=moved, transcendentals=0),
    )(*args)


def whole(shape):
    return pl.BlockSpec(shape, lambda *_: (0,) * len(shape))


def wide(ref, cell, times):
    channels, _, y_local, depth = ref.shape[1:]
    return jnp.concatenate([ref[t, :, cell].reshape(channels * y_local, depth) for t in times], axis=1)


def head_body(field_ref, table_ref, head_ref):
    def one(cell, carry):
        values = wide(field_ref, cell, range(field_ref.shape[0]))
        head_ref[cell] = dot(values, table_ref[...]).astype(jnp.bfloat16)
        return carry

    lax.fori_loop(0, field_ref.shape[2], one, 0)


def inner_body(field_ref, cot_ref, mid_ref, mix_ref, syn_ref, table_ref, grad_ref, head_ref):
    steps, channels, cells, y_local, depth = field_ref.shape

    def one(cell, carry):
        middle = mid_ref[cell]
        total = jnp.zeros(middle.shape, jnp.float32)
        for t in range(0, steps, 2):
            lanes = slice(t * depth, (t + 2) * depth)
            preact = dot(middle, syn_ref[:, lanes]) + dot(mix_ref[...], wide(field_ref, cell, (t, t + 1)))
            cot = wide(cot_ref, cell, (t, t + 1)).astype(jnp.float32)
            grad = (cot * gelu_slope(preact)).astype(jnp.bfloat16)
            for k in range(2):
                grad_ref[t + k, :, cell] = grad[:, k * depth : (k + 1) * depth].reshape(channels, y_local, depth)
            total += dot(grad, table_ref[lanes, :])
        head_ref[cell] = total.astype(jnp.bfloat16)
        return carry

    lax.fori_loop(0, cells, one, 0)


def outer_body(grad_ref, mid_ref, mix_ref, syn_ref, out_ref):
    steps, channels, cells, y_local, depth = grad_ref.shape

    def one(cell, carry):
        middle = mid_ref[cell]
        for t in range(0, steps, 2):
            lanes = slice(t * depth, (t + 2) * depth)
            total = dot(middle, syn_ref[:, lanes]) + dot(mix_ref[...], wide(grad_ref, cell, (t, t + 1)))
            total = total.astype(jnp.bfloat16)
            for k in range(2):
                out_ref[t + k, :, cell] = total[:, k * depth : (k + 1) * depth].reshape(channels, y_local, depth)
        return carry

    lax.fori_loop(0, cells, one, 0)


def y_down_body(rows_ref, table_ref, out_ref):
    owners, cells, channels, y_local, lanes = rows_ref.shape
    for c in range(channels):
        stacked = jnp.concatenate([rows_ref[s, x, c] for x in range(cells) for s in range(owners)], axis=0)
        out_ref[:, c] = dot(table_ref[...], stacked).astype(jnp.bfloat16).reshape(owners, -1, lanes)


def x_down_body(rows_ref, table_ref, out_ref):
    owners, channels, group, lanes = rows_ref.shape
    for c in range(channels):
        stacked = jnp.concatenate([rows_ref[s, c] for s in range(owners)], axis=0)
        done = dot(stacked, table_ref[...], 0, 0).astype(jnp.bfloat16)
        out_ref[:, c] = done.reshape(out_ref.shape[0], -1, done.shape[1])


def x_up_body(modes_ref, table_ref, out_ref):
    planes, channels, group, lanes = modes_ref.shape
    for c in range(channels):
        stacked = jnp.concatenate([modes_ref[d, c] for d in range(planes)], axis=0)
        done = dot(table_ref[...], stacked, 1, 1).astype(jnp.bfloat16)
        out_ref[:, c] = done.reshape(out_ref.shape[0], -1, done.shape[1])


def y_up_body(rows_ref, table_ref, out_ref):
    owners, channels, group, lanes = rows_ref.shape
    cells, y_local = out_ref.shape[1], out_ref.shape[3]
    for c in range(channels):
        stacked = jnp.concatenate([rows_ref[s, c] for s in range(owners)], axis=0)
        done = dot(table_ref[...], stacked).astype(jnp.bfloat16)
        for x in range(cells):
            for d in range(owners):
                start = (x * owners + d) * y_local
                out_ref[d, x, c] = done[start : start + y_local]


def shards(x_devices, y_devices, state_field, cotangent, spectral_weight, point_weight):
    steps, channels, x_local, y_local, depth = state_field.shape
    j_local, q_local = spectral_weight.shape[:2]
    time_modes, modes = spectral_weight.shape[4:]
    lanes = time_modes * modes
    rows = channels * y_local
    x_extent, y_extent = x_local * x_devices, y_local * y_devices
    bf16 = jnp.bfloat16

    x_pieces = math.gcd(x_local, y_devices)
    c_pieces = y_devices // x_pieces
    x_piece, c_piece = x_local // x_pieces, channels // c_pieces
    group = x_piece * j_local

    time_table, depth_table = basis(time_modes, steps), basis(modes, depth)
    x_table, y_table = basis(modes, x_extent), basis(modes, y_extent)
    synth = np.einsum("pt,qz->qptz", time_table, depth_table).reshape(lanes, steps * depth)
    y_mat = np.einsum("xw,djy->dxjwy", np.eye(x_piece), y_table.reshape(y_devices, j_local, y_extent))
    y_mat = y_mat.reshape(y_devices * group, x_piece * y_extent)
    x_mat = np.einsum("jk,igx->gxjki", np.eye(j_local), x_table.reshape(modes, x_devices, x_local))
    x_mat = x_mat.reshape(x_devices, x_local * j_local, j_local * modes)
    syn, ana = jnp.asarray(narrow(synth)), jnp.asarray(narrow(synth.T))
    y_mat, y_mat_t = jnp.asarray(narrow(y_mat)), jnp.asarray(narrow(y_mat.T))
    x_mat = lax.dynamic_index_in_dim(jnp.asarray(narrow(x_mat)), lax.axis_index("gx"), 0, keepdims=False)
    eye = jnp.eye(y_local, dtype=bf16)
    mix_up, mix_back = jnp.kron(point_weight.T, eye), jnp.kron(point_weight, eye)

    step = math.gcd(x_local, 4)
    grid = (x_local // step,)
    field_spec = pl.BlockSpec((steps, channels, step, y_local, depth), lambda g: (0, 0, g, 0, 0))
    head_spec = pl.BlockSpec((step, rows, lanes), lambda g: (g, 0, 0))
    head_shape = jax.ShapeDtypeStruct((x_local, rows, lanes), bf16)
    field_shape = jax.ShapeDtypeStruct(state_field.shape, bf16)
    field_bytes, head_bytes = 2 * state_field.size, 2 * x_local * rows * lanes
    head_flops = 2 * x_local * rows * lanes * steps * depth
    mix_flops = 2 * state_field.size * rows

    def small(body, out, values, table):
        shape = jax.ShapeDtypeStruct(out, bf16)
        return call(
            body, (1,), [whole(values.shape), whole(table.shape)], whole(out), shape,
            2 * values.size * 512, 2 * (values.size + math.prod(out)), (values, table),
        )

    def analyze(heads):
        heads = heads.reshape(y_devices, -1, lanes)
        heads = lax.all_to_all(heads, YZ, 0, 0, tiled=True)
        heads = heads.reshape(y_devices, x_piece, c_piece, y_local, lanes)
        part = small(y_down_body, (y_devices, c_piece, group, lanes), heads, y_mat)
        part = lax.all_to_all(part, YZ, 0, 0, tiled=True)
        part = part.reshape(x_pieces, channels, group, lanes)
        part = small(x_down_body, (x_devices, channels, q_local * time_modes, j_local * modes), part, x_mat)
        part = lax.all_to_all(part, "gx", 0, 0, tiled=True)
        return jnp.sum(part.astype(jnp.float32), axis=0).astype(bf16)

    def synthesize(spec):
        spec = lax.all_gather(spec, "gx", axis=0)
        part = small(x_up_body, (x_pieces, channels, group, lanes), spec, x_mat)
        part = part.reshape(y_devices, c_piece, group, lanes)
        part = lax.all_to_all(part, YZ, 0, 0, tiled=True)
        part = small(y_up_body, (y_devices, x_piece, c_piece, y_local, lanes), part, y_mat_t)
        part = lax.all_to_all(part.reshape(y_devices, -1, lanes), YZ, 0, 0, tiled=True)
        return part.reshape(x_local, rows, lanes)

    weight = jnp.transpose(spectral_weight, (2, 3, 1, 4, 0, 5))
    weight = weight.reshape(channels, channels, q_local * time_modes, j_local * modes)

    heads = call(
        head_body, grid, [field_spec, whole(ana.shape)], head_spec, head_shape,
        head_flops, field_bytes + head_bytes, (state_field, ana),
    )
    modes_in = analyze(heads).astype(jnp.float32)
    modes_out = jnp.sum(modes_in[:, None] * weight.astype(jnp.float32), axis=0).astype(bf16)
    grad_pre, heads = call(
        inner_body, grid,
        [field_spec, field_spec, head_spec, whole(mix_up.shape), whole(syn.shape), whole(ana.shape)],
        [field_spec, head_spec], [field_shape, head_shape],
        2 * head_flops + mix_flops, 3 * field_bytes + 2 * head_bytes,
        (state_field, cotangent, synthesize(modes_out), mix_up, syn, ana),
    )
    grad_modes = analyze(heads).astype(jnp.float32)
    grad_spectral = (modes_in[:, None] * grad_modes[None]).reshape(
        channels, channels, q_local, time_modes, j_local, modes
    )
    grad_spectral = jnp.transpose(grad_spectral, (4, 2, 0, 1, 3, 5))
    back_modes = jnp.sum(grad_modes[None] * weight.astype(jnp.float32), axis=1).astype(bf16)
    grad_field = call(
        outer_body, grid, [field_spec, head_spec, whole(mix_back.shape), whole(syn.shape)],
        field_spec, field_shape, head_flops + mix_flops, 2 * field_bytes + head_bytes,
        (grad_pre, synthesize(back_modes), mix_back, syn),
    )
    return grad_field, grad_spectral


def solution(mesh):
    in_specs = (
        P("parts", None, "gx", YZ, None),
        P("parts", None, "gx", YZ, None),
        P(YZ, "gx", None, None, None, None),
        P(),
    )
    out_specs = (
        P("parts", None, "gx", YZ, None),
        P(("parts",) + YZ, "gx", None, None, None, None),
    )
    body = functools.partial(shards, mesh.shape["gx"], mesh.shape["gy"] * mesh.shape["gz"])
    return jax.shard_map(body, mesh=mesh, in_specs=in_specs, out_specs=out_specs, check_vma=False)
```

```python
import functools
import math

import jax
import jax.numpy as jnp
import ml_dtypes
import numpy as np
from jax import lax
from jax.experimental import pallas as pl
from jax.experimental.pallas import tpu as pltpu
from jax.sharding import PartitionSpec as P

YZ = ("gy", "gz")
HALF_ROOT = 1.0 / math.sqrt(2.0)
DENSITY = 1.0 / math.sqrt(2.0 * math.pi)


def basis(row_count, extent):
    row = np.arange(row_count)[:, None]
    cell = np.arange(extent)[None, :]
    radians = ((row + 1) // 2 * cell % extent) * (2.0 * math.pi / extent)
    wave = np.where(row % 2 == 0, np.cos(radians), np.sin(radians))
    scale = np.where(row == 0, math.sqrt(1.0 / extent), math.sqrt(2.0 / extent))
    return (wave * scale).astype(ml_dtypes.bfloat16).astype(np.float32)


def narrow(table):
    return np.asarray(table, dtype=ml_dtypes.bfloat16)


def dot(left, right, left_dim=1, right_dim=0):
    return lax.dot_general(
        left, right, (((left_dim,), (right_dim,)), ((), ())), preferred_element_type=jnp.float32
    )


def gelu_slope(value):
    size = jnp.abs(value)
    bell = jnp.exp2(value * value * (-0.5 * math.log2(math.e)))
    span = 1.0 + (0.3275911 * HALF_ROOT) * size
    t = pl.reciprocal(span, approx=True)
    t = t * (2.0 - span * t)
    tail = t * (
        0.5 * 0.254829592
        + t * (0.5 * -0.284496736 + t * (0.5 * 1.421413741 + t * (0.5 * -1.453152027 + t * (0.5 * 1.061405429))))
    )
    low = bell * (tail - DENSITY * size)
    return jnp.where(value >= 0.0, 1.0 - low, low)


def call(body, grid, in_specs, out_specs, out_shape, flops, moved, args):
    return pl.pallas_call(
        body,
        grid=grid,
        in_specs=in_specs,
        out_specs=out_specs,
        out_shape=out_shape,
        compiler_params=pltpu.CompilerParams(vmem_limit_bytes=48 * 1024 * 1024),
        cost_estimate=pl.CostEstimate(flops=flops, bytes_accessed=moved, transcendentals=0),
    )(*args)


def whole(shape):
    return pl.BlockSpec(shape, lambda *_: (0,) * len(shape))


def wide(ref, cell, times):
    channels, _, y_local, depth = ref.shape[1:]
    return jnp.concatenate([ref[t, :, cell].reshape(channels * y_local, depth) for t in times], axis=1)


def head_body(field_ref, table_ref, head_ref):
    steps, _, cells, _, depth = field_ref.shape
    for cell in range(cells):
        total = 0.0
        for t in range(0, steps, 2):
            total += dot(wide(field_ref, cell, (t, t + 1)), table_ref[t * depth : (t + 2) * depth, :])
        head_ref[cell] = total.astype(jnp.bfloat16)


def inner_body(field_ref, cot_ref, mid_ref, mix_ref, syn_ref, table_ref, grad_ref, head_ref):
    steps, channels, cells, y_local, depth = field_ref.shape
    rows = channels * y_local
    band = math.gcd(rows, 32)
    for cell in range(cells):
        middle = mid_ref[cell]
        total = 0.0
        for t in range(0, steps, 2):
            lanes = slice(t * depth, (t + 2) * depth)
            preact = dot(middle, syn_ref[:, lanes]) + dot(mix_ref[...], wide(field_ref, cell, (t, t + 1)))
            cot = wide(cot_ref, cell, (t, t + 1))
            bands = []
            for r in range(0, rows, band):
                slope = gelu_slope(preact[r : r + band])
                bands.append((cot[r : r + band].astype(jnp.float32) * slope).astype(jnp.bfloat16))
            grad = jnp.concatenate(bands, axis=0)
            for k in range(2):
                grad_ref[t + k, :, cell] = grad[:, k * depth : (k + 1) * depth].reshape(channels, y_local, depth)
            total += dot(grad, table_ref[lanes, :])
        head_ref[cell] = total.astype(jnp.bfloat16)


def outer_body(grad_ref, mid_ref, mix_ref, syn_ref, out_ref):
    steps, channels, cells, y_local, depth = grad_ref.shape
    for cell in range(cells):
        middle = mid_ref[cell]
        for t in range(0, steps, 2):
            lanes = slice(t * depth, (t + 2) * depth)
            total = dot(middle, syn_ref[:, lanes]) + dot(mix_ref[...], wide(grad_ref, cell, (t, t + 1)))
            total = total.astype(jnp.bfloat16)
            for k in range(2):
                out_ref[t + k, :, cell] = total[:, k * depth : (k + 1) * depth].reshape(channels, y_local, depth)


def y_down_body(rows_ref, table_ref, out_ref):
    owners, cells = rows_ref.shape[:2]
    planes, _, groups, height, width = out_ref.shape
    members = rows_ref.shape[2] // groups
    span = width // members
    for k in range(groups):
        done = []
        for c in range(k * members, (k + 1) * members):
            stacked = jnp.concatenate([rows_ref[s, x, c] for x in range(cells) for s in range(owners)], axis=0)
            done.append(dot(table_ref[...], stacked).astype(jnp.bfloat16))
        for g in range(planes):
            piece = jnp.concatenate([part[:, g * span : (g + 1) * span] for part in done], axis=1)
            out_ref[g, :, k] = piece.reshape(owners, height, width)


def y_up_body(rows_ref, table_ref, out_ref):
    planes, owners, groups, _, width = rows_ref.shape
    _, cells, channels, y_local, _ = out_ref.shape
    members = channels // groups
    span = width // members
    for c in range(channels):
        lanes = slice(c % members * span, (c % members + 1) * span)
        stacked = jnp.concatenate(
            [
                jnp.concatenate([rows_ref[g, s, c // members][:, lanes] for g in range(planes)], axis=1)
                for s in range(owners)
            ],
            axis=0,
        )
        done = dot(table_ref[...], stacked).astype(jnp.bfloat16)
        for x in range(cells):
            for d in range(owners):
                start = (x * owners + d) * y_local
                out_ref[d, x, c] = done[start : start + y_local]


def spectral_body(back, rows_ref, table_ref, weight_ref, modes_ref, out_ref):
    planes, x_pieces, c_pieces, groups, height, width = rows_ref.shape
    channels, span, lanes = modes_ref.shape
    members = width // span
    for h in range(c_pieces):
        for k in range(groups):
            stacked = jnp.concatenate(
                [rows_ref[g, x, h, k] for g in range(planes) for x in range(x_pieces)], axis=0
            )
            first = (h * groups + k) * members
            done = dot(stacked, table_ref[...], 0, 0).astype(jnp.bfloat16)
            modes_ref[first : first + members] = done.reshape(members, span, lanes)
    for h in range(c_pieces):
        for k in range(groups):
            mixed = []
            for m in range(members):
                to = (h * groups + k) * members + m
                total = 0.0
                for of in range(channels):
                    weight = weight_ref[to, of] if back else weight_ref[of, to]
                    total += weight.astype(jnp.float32) * modes_ref[of].astype(jnp.float32)
                mixed.append(total.astype(jnp.bfloat16))
            done = dot(table_ref[...], jnp.concatenate(mixed, axis=0), 1, 1).astype(jnp.bfloat16)
            for g in range(planes):
                for x in range(x_pieces):
                    start = (g * x_pieces + x) * height
                    out_ref[g, x, h, k] = done[start : start + height]


def shards(x_devices, y_devices, state_field, cotangent, spectral_weight, point_weight):
    steps, channels, x_local, y_local, depth = state_field.shape
    j_local, q_local = spectral_weight.shape[:2]
    time_modes, modes = spectral_weight.shape[4:]
    lanes = time_modes * modes
    rows = channels * y_local
    x_extent, y_extent = x_local * x_devices, y_local * y_devices
    bf16 = jnp.bfloat16

    x_pieces = math.gcd(x_local, y_devices)
    c_pieces = y_devices // x_pieces
    x_piece, c_piece = x_local // x_pieces, channels // c_pieces
    group = x_piece * j_local

    time_table, depth_table = basis(time_modes, steps), basis(modes, depth)
    x_table, y_table = basis(modes, x_extent), basis(modes, y_extent)
    synth = np.einsum("pt,qz->qptz", time_table, depth_table).reshape(lanes, steps * depth)
    y_mat = np.einsum("xw,djy->dxjwy", np.eye(x_piece), y_table.reshape(y_devices, j_local, y_extent))
    y_mat = y_mat.reshape(y_devices * group, x_piece * y_extent)
    x_mat = np.einsum("jk,ix->xjki", np.eye(j_local), x_table).reshape(x_extent * j_local, j_local * modes)
    syn, ana, x_mat = jnp.asarray(narrow(synth)), jnp.asarray(narrow(synth.T)), jnp.asarray(narrow(x_mat))
    y_mat, y_mat_t = jnp.asarray(narrow(y_mat)), jnp.asarray(narrow(y_mat.T))
    eye = jnp.eye(y_local, dtype=bf16)
    mix_up, mix_back = jnp.kron(point_weight.T, eye), jnp.kron(point_weight, eye)

    step = math.gcd(x_local, 4)
    grid = (x_local // step,)
    field_spec = pl.BlockSpec((steps, channels, step, y_local, depth), lambda g: (0, 0, g, 0, 0))
    head_spec = pl.BlockSpec((step, rows, lanes), lambda g: (g, 0, 0))
    head_shape = jax.ShapeDtypeStruct((x_local, rows, lanes), bf16)
    field_shape = jax.ShapeDtypeStruct(state_field.shape, bf16)
    field_bytes, head_bytes = 2 * state_field.size, 2 * x_local * rows * lanes
    head_flops = 2 * x_local * rows * lanes * steps * depth
    mix_flops = 2 * state_field.size * rows

    def small(body, outs, values, *tables):
        shapes = [jax.ShapeDtypeStruct(out, bf16) for out in outs]
        return call(
            body, (1,), [whole(arg.shape) for arg in (values, *tables)], [whole(out) for out in outs], shapes,
            2 * values.size * 512, 4 * values.size, (values, *tables),
        )

    span = q_local * time_modes
    members = max(m for m in range(1, c_piece + 1) if c_piece % m == 0 and (m == 1 or m * span <= 128))
    packed = (x_devices, y_devices, c_piece // members, group, members * span)

    def exchange(pieces):
        shape = pieces.shape
        pieces = pieces.reshape((x_devices * y_devices,) + packed[2:])
        return lax.all_to_all(pieces, ("gx",) + YZ, 0, 0, tiled=True).reshape(shape)

    def spectral(back, heads, weight):
        heads = lax.all_to_all(heads.reshape(y_devices, -1, lanes), YZ, 0, 0, tiled=True)
        heads = heads.reshape(y_devices, x_piece, c_piece, y_local, lanes)
        (part,) = small(y_down_body, [packed], heads, y_mat)
        part = exchange(part).reshape((x_devices, x_pieces, c_pieces) + packed[2:])
        kept, part = small(
            functools.partial(spectral_body, back), [(channels, span, j_local * modes), part.shape], part, x_mat, weight
        )
        part = exchange(part).reshape(packed)
        (part,) = small(y_up_body, [(y_devices, x_piece, c_piece, y_local, lanes)], part, y_mat_t)
        part = lax.all_to_all(part.reshape(y_devices, -1, lanes), YZ, 0, 0, tiled=True)
        return part.reshape(x_local, rows, lanes), kept.astype(jnp.float32)

    weight = jnp.transpose(spectral_weight, (2, 3, 1, 4, 0, 5)).reshape(channels, channels, span, j_local * modes)

    heads = call(
        head_body, grid, [field_spec, whole(ana.shape)], head_spec, head_shape,
        head_flops, field_bytes + head_bytes, (state_field, ana),
    )
    middle, modes_in = spectral(False, heads, weight)
    grad_pre, heads = call(
        inner_body, grid,
        [field_spec, field_spec, head_spec, whole(mix_up.shape), whole(syn.shape), whole(ana.shape)],
        [field_spec, head_spec], [field_shape, head_shape],
        2 * head_flops + mix_flops, 3 * field_bytes + 2 * head_bytes,
        (state_field, cotangent, middle, mix_up, syn, ana),
    )
    middle, grad_modes = spectral(True, heads, weight)
    grad_spectral = (modes_in[:, None] * grad_modes[None]).reshape(
        channels, channels, q_local, time_modes, j_local, modes
    )
    grad_spectral = jnp.transpose(grad_spectral, (4, 2, 0, 1, 3, 5))
    grad_field = call(
        outer_body, grid, [field_spec, head_spec, whole(mix_back.shape), whole(syn.shape)],
        field_spec, field_shape, head_flops + mix_flops, 2 * field_bytes + head_bytes,
        (grad_pre, middle, mix_back, syn),
    )
    return grad_field, grad_spectral


def solution(mesh):
    in_specs = (
        P("parts", None, "gx", YZ, None),
        P("parts", None, "gx", YZ, None),
        P(YZ, "gx", None, None, None, None),
        P(),
    )
    out_specs = (
        P("parts", None, "gx", YZ, None),
        P(("parts",) + YZ, "gx", None, None, None, None),
    )
    body = functools.partial(shards, mesh.shape["gx"], mesh.shape["gy"] * mesh.shape["gz"])
    return jax.shard_map(body, mesh=mesh, in_specs=in_specs, out_specs=out_specs, check_vma=False)
```

```python
import functools
import math

import jax
import jax.numpy as jnp
import ml_dtypes
import numpy as np
from jax import lax
from jax.experimental import pallas as pl
from jax.experimental.pallas import tpu as pltpu
from jax.sharding import PartitionSpec as P

YZ = ("gy", "gz")
HALF_ROOT = 1.0 / math.sqrt(2.0)
DENSITY = 1.0 / math.sqrt(2.0 * math.pi)


def basis(row_count, extent):
    row = np.arange(row_count)[:, None]
    cell = np.arange(extent)[None, :]
    radians = ((row + 1) // 2 * cell % extent) * (2.0 * math.pi / extent)
    wave = np.where(row % 2 == 0, np.cos(radians), np.sin(radians))
    scale = np.where(row == 0, math.sqrt(1.0 / extent), math.sqrt(2.0 / extent))
    return (wave * scale).astype(ml_dtypes.bfloat16).astype(np.float32)


def narrow(table):
    return np.asarray(table, dtype=ml_dtypes.bfloat16)


def dot(left, right, left_dim=1, right_dim=0):
    return lax.dot_general(
        left, right, (((left_dim,), (right_dim,)), ((), ())), preferred_element_type=jnp.float32
    )


def gelu_slope(value):
    size = jnp.abs(value)
    bell = jnp.exp2(value * value * (-0.5 * math.log2(math.e)))
    span = 1.0 + (0.3275911 * HALF_ROOT) * size
    t = pl.reciprocal(span, approx=True)
    t = t * (2.0 - span * t)
    tail = t * (
        0.5 * 0.254829592
        + t * (0.5 * -0.284496736 + t * (0.5 * 1.421413741 + t * (0.5 * -1.453152027 + t * (0.5 * 1.061405429))))
    )
    low = bell * (tail - DENSITY * size)
    return jnp.where(value >= 0.0, 1.0 - low, low)


def call(body, grid, in_specs, out_specs, out_shape, flops, moved, args, order=None, scratch=(), aliases={}):
    spec = pltpu.PrefetchScalarGridSpec(
        num_scalar_prefetch=0 if order is None else 1,
        grid=grid,
        in_specs=in_specs,
        out_specs=out_specs,
        scratch_shapes=scratch,
    )
    return pl.pallas_call(
        body,
        grid_spec=spec,
        out_shape=out_shape,
        input_output_aliases=aliases,
        compiler_params=pltpu.CompilerParams(vmem_limit_bytes=48 * 1024 * 1024),
        cost_estimate=pl.CostEstimate(flops=int(flops), bytes_accessed=int(moved), transcendentals=0),
    )(*(() if order is None else (order,)), *args)


def whole(shape):
    return pl.BlockSpec(shape, lambda *_: (0,) * len(shape))


def wide(ref, cell, times):
    channels, _, y_local, depth = ref.shape[1:]
    return jnp.concatenate([ref[t, :, cell].reshape(channels * y_local, depth) for t in times], axis=1)


def admit(held, pieces, sub):
    for e, piece in enumerate(pieces):

        @pl.when(pl.program_id(0) == e * sub)
        def _(piece=piece):
            held[...] = piece[...]


def release(held, pieces, sub):
    for e, piece in enumerate(pieces):

        @pl.when(pl.program_id(0) == e * sub + sub - 1)
        def _(piece=piece):
            piece[...] = held[...]


def own_cells(sub, cells):
    return pl.ds(lax.rem(pl.program_id(0), sub) * cells, cells)


def head_body(sub, order_ref, field_ref, table_ref, *refs):
    heads, held = refs[:-1], refs[-1]
    steps, _, cells, _, depth = field_ref.shape
    total = 0.0
    for t in range(0, steps, 2):
        values = jnp.concatenate([wide(field_ref, cell, (t, t + 1)) for cell in range(cells)], axis=0)
        total += dot(values, table_ref[t * depth : (t + 2) * depth, :])
    held[own_cells(sub, cells)] = total.astype(jnp.bfloat16).reshape((cells,) + held.shape[1:])
    release(held, heads, sub)


def inner_body(sub, count, order_ref, field_ref, cot_ref, mix_ref, syn_ref, table_ref, *refs):
    mids, grad_ref, heads, (mid_held, head_held) = refs[:count], refs[count], refs[count + 1 : -2], refs[-2:]
    steps, channels, cells, y_local, depth = field_ref.shape
    rows = channels * y_local
    band = math.gcd(rows, 32)
    admit(mid_held, mids, sub)
    middle = mid_held[own_cells(sub, cells)].reshape(cells * rows, -1)
    total = 0.0
    for t in range(0, steps, 2):
        lanes = slice(t * depth, (t + 2) * depth)
        spread = dot(middle, syn_ref[:, lanes])
        bands = []
        for cell in range(cells):
            preact = spread[cell * rows : (cell + 1) * rows] + dot(mix_ref[...], wide(field_ref, cell, (t, t + 1)))
            cot = wide(cot_ref, cell, (t, t + 1))
            for r in range(0, rows, band):
                slope = gelu_slope(preact[r : r + band])
                bands.append((cot[r : r + band].astype(jnp.float32) * slope).astype(jnp.bfloat16))
        grad = jnp.concatenate(bands, axis=0)
        for cell in range(cells):
            for k in range(2):
                part = grad[cell * rows : (cell + 1) * rows, k * depth : (k + 1) * depth]
                grad_ref[t + k, :, cell] = part.reshape(channels, y_local, depth)
        total += dot(grad, table_ref[lanes, :])
    head_held[own_cells(sub, cells)] = total.astype(jnp.bfloat16).reshape((cells,) + head_held.shape[1:])
    release(head_held, heads, sub)


def outer_body(sub, count, order_ref, grad_ref, mix_ref, syn_ref, *refs):
    mids, out_ref, mid_held = refs[:count], refs[-2], refs[-1]
    steps, channels, cells, y_local, depth = grad_ref.shape
    rows = channels * y_local
    admit(mid_held, mids, sub)
    middle = mid_held[own_cells(sub, cells)].reshape(cells * rows, -1)
    for t in range(0, steps, 2):
        spread = dot(middle, syn_ref[:, t * depth : (t + 2) * depth])
        for cell in range(cells):
            total = spread[cell * rows : (cell + 1) * rows] + dot(mix_ref[...], wide(grad_ref, cell, (t, t + 1)))
            total = total.astype(jnp.bfloat16)
            for k in range(2):
                out_ref[t + k, :, cell] = total[:, k * depth : (k + 1) * depth].reshape(channels, y_local, depth)


def y_down_body(table_ref, *refs):
    pieces, out_ref = refs[:-1], refs[-1]
    cells, channels = pieces[0].shape[:2]
    planes, owners, groups, height, width = out_ref.shape
    members = channels // groups
    span = width // members
    for k in range(groups):
        done = []
        for c in range(k * members, (k + 1) * members):
            stacked = jnp.concatenate([piece[x, c] for piece in pieces for x in range(cells)], axis=0)
            done.append(dot(table_ref[...], stacked).astype(jnp.bfloat16))
        for g in range(planes):
            piece = jnp.concatenate([part[:, g * span : (g + 1) * span] for part in done], axis=1)
            out_ref[g, :, k] = piece.reshape(owners, height, width)


def y_up_body(rows_ref, table_ref, *pieces):
    planes, owners, groups, _, width = rows_ref.shape
    cells, channels, y_local, _ = pieces[0].shape
    members = channels // groups
    span = width // members
    for c in range(channels):
        lanes = slice(c % members * span, (c % members + 1) * span)
        stacked = jnp.concatenate(
            [
                jnp.concatenate([rows_ref[g, s, c // members][:, lanes] for g in range(planes)], axis=1)
                for s in range(owners)
            ],
            axis=0,
        )
        done = dot(table_ref[...], stacked).astype(jnp.bfloat16)
        for k, piece in enumerate(pieces):
            for x in range(cells):
                start = (k * cells + x) * y_local
                piece[x, c] = done[start : start + y_local]


def spectral_body(back, rows_ref, table_ref, weight_ref, modes_ref, out_ref):
    planes, x_pieces, c_pieces, groups, height, width = rows_ref.shape
    channels, span, lanes = modes_ref.shape
    members = width // span
    for h in range(c_pieces):
        for k in range(groups):
            stacked = jnp.concatenate(
                [rows_ref[g, x, h, k] for g in range(planes) for x in range(x_pieces)], axis=0
            )
            first = (h * groups + k) * members
            done = dot(stacked, table_ref[...], 0, 0).astype(jnp.bfloat16)
            modes_ref[first : first + members] = done.reshape(members, span, lanes)
    for h in range(c_pieces):
        for k in range(groups):
            mixed = []
            for m in range(members):
                to = (h * groups + k) * members + m
                total = 0.0
                for of in range(channels):
                    weight = weight_ref[to, of] if back else weight_ref[of, to]
                    total += weight.astype(jnp.float32) * modes_ref[of].astype(jnp.float32)
                mixed.append(total.astype(jnp.bfloat16))
            done = dot(table_ref[...], jnp.concatenate(mixed, axis=0), 1, 1).astype(jnp.bfloat16)
            for g in range(planes):
                for x in range(x_pieces):
                    start = (g * x_pieces + x) * height
                    out_ref[g, x, h, k] = done[start : start + height]


def shards(x_devices, y_devices, state_field, cotangent, spectral_weight, point_weight):
    steps, channels, x_local, y_local, depth = state_field.shape
    j_local, q_local = spectral_weight.shape[:2]
    time_modes, modes = spectral_weight.shape[4:]
    lanes = time_modes * modes
    rows = channels * y_local
    x_extent, y_extent = x_local * x_devices, y_local * y_devices
    bf16 = jnp.bfloat16

    x_pieces = math.gcd(x_local, y_devices)
    c_pieces = y_devices // x_pieces
    x_piece, c_piece = x_local // x_pieces, channels // c_pieces
    group = x_piece * j_local

    paired = c_pieces == 1 and y_devices & (y_devices - 1) == 0
    blocks = x_pieces
    me = lax.axis_index(YZ)
    order = jnp.arange(blocks, dtype=jnp.int32) ^ (me.astype(jnp.int32) if paired else 0)

    time_table, depth_table = basis(time_modes, steps), basis(modes, depth)
    x_table, y_table = basis(modes, x_extent), basis(modes, y_extent)
    synth = np.einsum("pt,qz->qptz", time_table, depth_table).reshape(lanes, steps * depth)
    y_mat = np.einsum("xw,djsy->dxjswy", np.eye(x_piece), y_table.reshape(y_devices, j_local, y_devices, y_local))
    y_mat = y_mat.reshape(y_devices * group, y_devices, x_piece * y_local)
    seen = [[d ^ k if paired else k for k in range(y_devices)] for d in range(y_devices if paired else 1)]
    y_mats = np.stack([y_mat[:, owners].reshape(y_devices * group, -1) for owners in seen])
    mine = me if paired else 0
    x_mat = np.einsum("jk,ix->xjki", np.eye(j_local), x_table).reshape(x_extent * j_local, j_local * modes)
    syn, ana, x_mat = jnp.asarray(narrow(synth)), jnp.asarray(narrow(synth.T)), jnp.asarray(narrow(x_mat))
    y_mat = lax.dynamic_index_in_dim(jnp.asarray(narrow(y_mats)), mine, 0, keepdims=False)
    y_mat_t = lax.dynamic_index_in_dim(jnp.asarray(narrow(y_mats.swapaxes(1, 2))), mine, 0, keepdims=False)
    eye = jnp.eye(y_local, dtype=bf16)
    mix_up, mix_back = jnp.kron(point_weight.T, eye), jnp.kron(point_weight, eye)

    step = math.gcd(x_piece, 2)
    sub = x_piece // step
    block_field = jax.ShapeDtypeStruct((steps, channels, x_piece, y_local, depth), bf16)
    block_head = jax.ShapeDtypeStruct((x_piece, rows, lanes), bf16)
    field_bytes, head_bytes = 2 * math.prod(block_field.shape), 2 * math.prod(block_head.shape)
    head_flops, mix_flops = head_bytes * steps * depth, field_bytes * rows
    held = pltpu.VMEM(block_head.shape, bf16)

    def grouped(first):
        where = lambda g, order: (0, 0, order[first + g // sub] * sub + g % sub, 0, 0)
        return pl.BlockSpec((steps, channels, step, y_local, depth), where)

    in_group = pl.BlockSpec((steps, channels, step, y_local, depth), lambda g, order: (0, 0, g, 0, 0))
    pairs = [(k, min(2, blocks - k)) for k in range(0, blocks, 2)]
    groups = [(0, 1)] + pairs[1:] + [(1, 1)] if blocks > 1 else pairs

    def head_call(first, count):
        return call(
            functools.partial(head_body, sub), (count * sub,), [grouped(first), whole(ana.shape)],
            [whole(block_head.shape)] * count, [block_head] * count,
            count * head_flops, count * (field_bytes + head_bytes), (state_field, ana), order, [held],
        )

    def inner_call(first, count, middle):
        grads = (steps, channels, count * x_piece, y_local, depth)
        tables = (mix_up, syn, ana)
        done = call(
            functools.partial(inner_body, sub, count), (count * sub,),
            [grouped(first)] * 2 + [whole(arg.shape) for arg in tables] + [whole(block_head.shape)] * count,
            [in_group] + [whole(block_head.shape)] * count,
            [jax.ShapeDtypeStruct(grads, bf16)] + [block_head] * count,
            2 * count * (2 * head_flops + mix_flops), count * (3 * field_bytes + 2 * head_bytes),
            (state_field, cotangent, *tables, *middle[first : first + count]), order, [held, held],
        )
        return done[0], done[1:]

    def outer_call(first, count, grads, middle, field):
        tables = (mix_back, syn)
        return call(
            functools.partial(outer_body, sub, count), (count * sub,),
            [in_group] + [whole(arg.shape) for arg in tables] + [whole(block_head.shape)] * count
            + [pl.BlockSpec(memory_space=pl.ANY)] * len(field),
            grouped(first), jax.ShapeDtypeStruct(state_field.shape, bf16),
            count * (head_flops + mix_flops), count * (2 * field_bytes + head_bytes),
            (grads, *tables, *middle[first : first + count], *field), order, [held],
            {4 + count: 0} if field else {},
        )

    def small(body, outs, *args):
        shapes = [jax.ShapeDtypeStruct(out, bf16) for out in outs]
        size = sum(arg.size for arg in args)
        return call(
            body, (1,), [whole(arg.shape) for arg in args], [whole(out) for out in outs], shapes, 1024 * size, 4 * size, args
        )

    span = q_local * time_modes
    members = max(m for m in range(1, c_piece + 1) if c_piece % m == 0 and (m == 1 or m * span <= 128))
    packed = (x_devices, y_devices, c_piece // members, group, members * span)

    def exchange(pieces):
        shape = pieces.shape
        pieces = pieces.reshape((x_devices * y_devices,) + packed[2:])
        return lax.all_to_all(pieces, ("gx",) + YZ, 0, 0, tiled=True).reshape(shape)

    def swap(pieces, count, shape):
        if paired:
            pairs = [[(d, d ^ k) for d in range(y_devices)] for k in range(y_devices)]
            pieces = [lax.ppermute(piece, YZ, pairs[k]) if k else piece for k, piece in enumerate(pieces)]
        else:
            pieces = jnp.stack(pieces).reshape(y_devices, -1, lanes)
            pieces = lax.all_to_all(pieces, YZ, 0, 0, tiled=True).reshape((count,) + shape)
        return [pieces[k].reshape(shape) for k in range(count)]

    def spectral(back, heads, weight):
        cells = (x_piece, c_piece, y_local, lanes)
        (part,) = small(y_down_body, [packed], y_mat, *swap(heads, y_devices, cells))
        part = exchange(part).reshape((x_devices, x_pieces, c_pieces) + packed[2:])
        kept, part = small(
            functools.partial(spectral_body, back), [(channels, span, j_local * modes), part.shape], part, x_mat, weight
        )
        part = exchange(part).reshape(packed)
        pieces = small(y_up_body, [cells] * y_devices, part, y_mat_t)
        return swap(pieces, blocks, block_head.shape), kept.astype(jnp.float32)

    weight = jnp.transpose(spectral_weight, (2, 3, 1, 4, 0, 5)).reshape(channels, channels, span, j_local * modes)

    heads = [None] * blocks
    for first, count in reversed(pairs):
        heads[first : first + count] = head_call(first, count)
    middle, modes_in = spectral(False, heads, weight)
    grads = {}
    for first, count in groups:
        grads[first], heads[first : first + count] = inner_call(first, count, middle)
    middle, grad_modes = spectral(True, heads, weight)
    grad_spectral = (modes_in[:, None] * grad_modes[None]).reshape(
        channels, channels, q_local, time_modes, j_local, modes
    )
    grad_spectral = jnp.transpose(grad_spectral, (4, 2, 0, 1, 3, 5))
    field = ()
    for first, count in sorted(groups):
        field = (outer_call(first, count, grads[first], middle, field),)
    return field[0], grad_spectral


def solution(mesh):
    in_specs = (
        P("parts", None, "gx", YZ, None),
        P("parts", None, "gx", YZ, None),
        P(YZ, "gx", None, None, None, None),
        P(),
    )
    out_specs = (
        P("parts", None, "gx", YZ, None),
        P(("parts",) + YZ, "gx", None, None, None, None),
    )
    body = functools.partial(shards, mesh.shape["gx"], mesh.shape["gy"] * mesh.shape["gz"])
    return jax.shard_map(body, mesh=mesh, in_specs=in_specs, out_specs=out_specs, check_vma=False)
```

```python
import functools
import math

import jax
import jax.numpy as jnp
import ml_dtypes
import numpy as np
from jax import lax
from jax.experimental import pallas as pl
from jax.experimental.pallas import tpu as pltpu
from jax.sharding import PartitionSpec as P

YZ = ("gy", "gz")
HALF_ROOT = 1.0 / math.sqrt(2.0)
DENSITY = 1.0 / math.sqrt(2.0 * math.pi)


def basis(row_count, extent):
    row = np.arange(row_count)[:, None]
    cell = np.arange(extent)[None, :]
    radians = ((row + 1) // 2 * cell % extent) * (2.0 * math.pi / extent)
    wave = np.where(row % 2 == 0, np.cos(radians), np.sin(radians))
    scale = np.where(row == 0, math.sqrt(1.0 / extent), math.sqrt(2.0 / extent))
    return (wave * scale).astype(ml_dtypes.bfloat16).astype(np.float32)


def narrow(table):
    return np.asarray(table, dtype=ml_dtypes.bfloat16)


def dot(left, right, left_dim=1, right_dim=0):
    return lax.dot_general(
        left, right, (((left_dim,), (right_dim,)), ((), ())), preferred_element_type=jnp.float32
    )


def gelu_slope(value):
    size = jnp.abs(value)
    bell = jnp.exp2(value * value * (-0.5 * math.log2(math.e)))
    span = 1.0 + (0.3275911 * HALF_ROOT) * size
    t = pl.reciprocal(span, approx=True)
    t = t * (2.0 - span * t)
    tail = t * (
        0.5 * 0.254829592
        + t * (0.5 * -0.284496736 + t * (0.5 * 1.421413741 + t * (0.5 * -1.453152027 + t * (0.5 * 1.061405429))))
    )
    low = bell * (tail - DENSITY * size)
    return jnp.where(value >= 0.0, 1.0 - low, low)


ANY = pl.BlockSpec(memory_space=pl.ANY)


def call(body, grid, in_specs, out_specs, out_shape, flops, moved, args, order=None, scratch=(), aliases={}, after=()):
    lead = 0 if order is None else 1
    count = lead + len(args)

    def placed(*refs):
        body(*refs[:count], *refs[count + len(after) :])

    spec = pltpu.PrefetchScalarGridSpec(
        num_scalar_prefetch=lead,
        grid=grid,
        in_specs=list(in_specs) + [ANY] * len(after),
        out_specs=out_specs,
        scratch_shapes=scratch,
    )
    return pl.pallas_call(
        placed,
        grid_spec=spec,
        out_shape=out_shape,
        input_output_aliases={lead + operand: out for operand, out in aliases.items()},
        compiler_params=pltpu.CompilerParams(vmem_limit_bytes=60 * 1024 * 1024),
        cost_estimate=pl.CostEstimate(flops=int(flops), bytes_accessed=int(moved), transcendentals=0),
    )(*(() if order is None else (order,)), *args, *after)


def whole(shape):
    return pl.BlockSpec(shape, lambda *_: (0,) * len(shape))


def wide(ref, cell, times):
    channels, _, y_local, depth = ref.shape[1:]
    return jnp.concatenate([ref[t, :, cell].reshape(channels * y_local, depth) for t in times], axis=1)


def admit(held, pieces, sub):
    for e, piece in enumerate(pieces):

        @pl.when(pl.program_id(0) == e * sub)
        def _(piece=piece):
            held[...] = piece[...]


def release(held, pieces, sub):
    for e, piece in enumerate(pieces):

        @pl.when(pl.program_id(0) == e * sub + sub - 1)
        def _(piece=piece):
            piece[...] = held[...]


def own_cells(sub, cells):
    return pl.ds(lax.rem(pl.program_id(0), sub) * cells, cells)


def head_body(sub, order_ref, field_ref, table_ref, *refs):
    heads, held = refs[:-1], refs[-1]
    steps, _, cells, _, depth = field_ref.shape
    first = lax.rem(pl.program_id(0), sub) * cells
    for cell in range(cells):
        total = 0.0
        for t in range(0, steps, 2):
            total += dot(wide(field_ref, cell, (t, t + 1)), table_ref[t * depth : (t + 2) * depth, :])
        held[first + cell] = total.astype(jnp.bfloat16)
    release(held, heads, sub)


def inner_body(sub, count, order_ref, field_ref, cot_ref, mix_ref, syn_ref, table_ref, *refs):
    mids, (grad_ref, *heads), (mid_held, head_held) = refs[:count], refs[-count - 3 : -2], refs[-2:]
    steps, channels, cells, y_local, depth = field_ref.shape
    rows = channels * y_local
    band = math.gcd(rows, 32)
    admit(mid_held, mids, sub)
    middle = mid_held[own_cells(sub, cells)].reshape(cells * rows, -1)
    total = 0.0
    for t in range(0, steps, 2):
        lanes = slice(t * depth, (t + 2) * depth)
        spread = dot(middle, syn_ref[:, lanes])
        bands = []
        for cell in range(cells):
            preact = spread[cell * rows : (cell + 1) * rows] + dot(mix_ref[...], wide(field_ref, cell, (t, t + 1)))
            cot = wide(cot_ref, cell, (t, t + 1))
            for r in range(0, rows, band):
                slope = gelu_slope(preact[r : r + band])
                bands.append((cot[r : r + band].astype(jnp.float32) * slope).astype(jnp.bfloat16))
        grad = jnp.concatenate(bands, axis=0)
        for cell in range(cells):
            for k in range(2):
                part = grad[cell * rows : (cell + 1) * rows, k * depth : (k + 1) * depth]
                grad_ref[t + k, :, cell] = part.reshape(channels, y_local, depth)
        total += dot(grad, table_ref[lanes, :])
    head_held[own_cells(sub, cells)] = total.astype(jnp.bfloat16).reshape((cells,) + head_held.shape[1:])
    release(head_held, heads, sub)


def outer_body(sub, count, order_ref, grad_ref, mix_ref, syn_ref, *refs):
    mids, out_ref, mid_held = refs[:count], refs[-2], refs[-1]
    steps, channels, cells, y_local, depth = grad_ref.shape
    rows = channels * y_local
    admit(mid_held, mids, sub)
    middle = mid_held[own_cells(sub, cells)].reshape(cells * rows, -1)
    for t in range(0, steps, 2):
        spread = dot(middle, syn_ref[:, t * depth : (t + 2) * depth])
        for cell in range(cells):
            total = spread[cell * rows : (cell + 1) * rows] + dot(mix_ref[...], wide(grad_ref, cell, (t, t + 1)))
            total = total.astype(jnp.bfloat16)
            for k in range(2):
                out_ref[t + k, :, cell] = total[:, k * depth : (k + 1) * depth].reshape(channels, y_local, depth)


def y_down_body(table_ref, *refs):
    pieces, out_ref = refs[:-1], refs[-1]
    cells, channels = pieces[0].shape[:2]
    planes, owners, groups, height, width = out_ref.shape
    members = channels // groups
    span = width // members
    for k in range(groups):
        done = []
        for c in range(k * members, (k + 1) * members):
            stacked = jnp.concatenate([piece[x, c] for piece in pieces for x in range(cells)], axis=0)
            done.append(dot(table_ref[...], stacked).astype(jnp.bfloat16))
        for g in range(planes):
            piece = jnp.concatenate([part[:, g * span : (g + 1) * span] for part in done], axis=1)
            out_ref[g, :, k] = piece.reshape(owners, height, width)


def y_up_body(rows_ref, table_ref, *pieces):
    planes, owners, groups, _, width = rows_ref.shape
    cells, channels, y_local, _ = pieces[0].shape
    members = channels // groups
    span = width // members
    for c in range(channels):
        lanes = slice(c % members * span, (c % members + 1) * span)
        stacked = jnp.concatenate(
            [
                jnp.concatenate([rows_ref[g, s, c // members][:, lanes] for g in range(planes)], axis=1)
                for s in range(owners)
            ],
            axis=0,
        )
        done = dot(table_ref[...], stacked).astype(jnp.bfloat16)
        for k, piece in enumerate(pieces):
            for x in range(cells):
                start = (k * cells + x) * y_local
                piece[x, c] = done[start : start + y_local]


def spectral_body(back, rows_ref, table_ref, weight_ref, modes_ref, out_ref):
    planes, x_pieces, c_pieces, groups, height, width = rows_ref.shape
    channels, span, lanes = modes_ref.shape
    members = width // span
    for h in range(c_pieces):
        for k in range(groups):
            stacked = jnp.concatenate(
                [rows_ref[g, x, h, k] for g in range(planes) for x in range(x_pieces)], axis=0
            )
            first = (h * groups + k) * members
            done = dot(stacked, table_ref[...], 0, 0).astype(jnp.bfloat16)
            modes_ref[first : first + members] = done.reshape(members, span, lanes)
    for h in range(c_pieces):
        for k in range(groups):
            mixed = []
            for m in range(members):
                to = (h * groups + k) * members + m
                total = 0.0
                for of in range(channels):
                    weight = weight_ref[to, of] if back else weight_ref[of, to]
                    total += weight.astype(jnp.float32) * modes_ref[of].astype(jnp.float32)
                mixed.append(total.astype(jnp.bfloat16))
            done = dot(table_ref[...], jnp.concatenate(mixed, axis=0), 1, 1).astype(jnp.bfloat16)
            for g in range(planes):
                for x in range(x_pieces):
                    start = (g * x_pieces + x) * height
                    out_ref[g, x, h, k] = done[start : start + height]


def outer_product_body(left_ref, right_ref, out_ref):
    _, q_local, channels, _, time_modes, modes = out_ref.shape
    for j in range(left_ref.shape[2] // modes):

        @pl.when(pl.program_id(0) == j)
        def _(j=j):
            lanes = slice(j * modes, (j + 1) * modes)
            left = left_ref[:, :, lanes].astype(jnp.float32)
            right = right_ref[:, :, lanes].astype(jnp.float32)
            for q in range(q_local):
                rows = slice(q * time_modes, (q + 1) * time_modes)
                for c in range(channels):
                    out_ref[0, q, c] = left[c, rows] * right[:, rows]


def shards(x_devices, y_devices, state_field, cotangent, spectral_weight, point_weight):
    steps, channels, x_local, y_local, depth = state_field.shape
    j_local, q_local = spectral_weight.shape[:2]
    time_modes, modes = spectral_weight.shape[4:]
    lanes = time_modes * modes
    rows = channels * y_local
    x_extent, y_extent = x_local * x_devices, y_local * y_devices
    bf16 = jnp.bfloat16

    x_pieces = math.gcd(x_local, y_devices)
    c_pieces = y_devices // x_pieces
    x_piece, c_piece = x_local // x_pieces, channels // c_pieces
    group = x_piece * j_local

    paired = c_pieces == 1 and y_devices & (y_devices - 1) == 0
    blocks = x_pieces
    me = lax.axis_index(YZ)
    order = jnp.arange(blocks, dtype=jnp.int32) ^ (me.astype(jnp.int32) if paired else 0)

    time_table, depth_table = basis(time_modes, steps), basis(modes, depth)
    x_table, y_table = basis(modes, x_extent), basis(modes, y_extent)
    synth = np.einsum("pt,qz->qptz", time_table, depth_table).reshape(lanes, steps * depth)
    y_mat = np.einsum("xw,djsy->dxjswy", np.eye(x_piece), y_table.reshape(y_devices, j_local, y_devices, y_local))
    y_mat = y_mat.reshape(y_devices * group, y_devices, x_piece * y_local)
    seen = [[d ^ k if paired else k for k in range(y_devices)] for d in range(y_devices if paired else 1)]
    y_mats = np.stack([y_mat[:, owners].reshape(y_devices * group, -1) for owners in seen])
    mine = me if paired else 0
    x_mat = np.einsum("jk,ix->xjki", np.eye(j_local), x_table).reshape(x_extent * j_local, j_local * modes)
    syn, ana, x_mat = jnp.asarray(narrow(synth)), jnp.asarray(narrow(synth.T)), jnp.asarray(narrow(x_mat))
    y_mat = lax.dynamic_index_in_dim(jnp.asarray(narrow(y_mats)), mine, 0, keepdims=False)
    y_mat_t = lax.dynamic_index_in_dim(jnp.asarray(narrow(y_mats.swapaxes(1, 2))), mine, 0, keepdims=False)
    eye = jnp.eye(y_local, dtype=bf16)
    mix_up, mix_back = jnp.kron(point_weight.T, eye), jnp.kron(point_weight, eye)

    block_head = jax.ShapeDtypeStruct((x_piece, rows, lanes), bf16)
    full_field = jax.ShapeDtypeStruct(state_field.shape, bf16)
    field_bytes, head_bytes = 2 * state_field.size // blocks, 2 * math.prod(block_head.shape)
    head_flops, mix_flops = head_bytes * steps * depth, field_bytes * rows
    held = pltpu.VMEM(block_head.shape, bf16)
    head_step, step = math.gcd(x_piece, 4), math.gcd(x_piece, 2)

    def grouped(first, step):
        sub = x_piece // step
        where = lambda g, order: (0, 0, order[first + g // sub] * sub + g % sub, 0, 0)
        return pl.BlockSpec((steps, channels, step, y_local, depth), where)

    pairs = [(k, min(2, blocks - k)) for k in range(0, blocks, 2)]
    groups = [(0, 1)] + pairs[1:] + [(1, 1)] if blocks > 1 else pairs

    def head_call(first, count, after):
        sub = x_piece // head_step
        return call(
            functools.partial(head_body, sub), (count * sub,), [grouped(first, head_step), whole(ana.shape)],
            [whole(block_head.shape)] * count, [block_head] * count,
            count * head_flops, count * (field_bytes + head_bytes), (state_field, ana), order, [held], after=after,
        )

    def inner_call(first, count, middle, grads):
        sub = x_piece // step
        tables = (mix_up, syn, ana)
        spec = grouped(first, step)
        done = call(
            functools.partial(inner_body, sub, count), (count * sub,),
            [spec] * 2 + [whole(arg.shape) for arg in tables] + [whole(block_head.shape)] * count + [ANY] * len(grads),
            [spec] + [whole(block_head.shape)] * count, [full_field] + [block_head] * count,
            2 * count * (2 * head_flops + mix_flops), count * (3 * field_bytes + 2 * head_bytes),
            (state_field, cotangent, *tables, *middle[first : first + count], *grads), order, [held, held],
            {5 + count: 0} if grads else {},
        )
        return done[:1], done[1:]

    def outer_call(first, count, middle, grads, field):
        sub = x_piece // step
        tables = (mix_back, syn)
        spec = grouped(first, step)
        return call(
            functools.partial(outer_body, sub, count), (count * sub,),
            [spec] + [whole(arg.shape) for arg in tables] + [whole(block_head.shape)] * count + [ANY] * len(field),
            [spec], [full_field], count * (head_flops + mix_flops), count * (2 * field_bytes + head_bytes),
            (*grads, *tables, *middle[first : first + count], *field), order, [held],
            {3 + count: 0} if field else {},
        )

    def small(body, outs, *args, after=()):
        shapes = [jax.ShapeDtypeStruct(out, bf16) for out in outs]
        size = sum(arg.size for arg in args)
        return call(
            body, (1,), [whole(arg.shape) for arg in args], [whole(out) for out in outs], shapes, 1024 * size, 4 * size, args,
            after=after,
        )

    span = q_local * time_modes
    members = max(m for m in range(1, c_piece + 1) if c_piece % m == 0 and (m == 1 or m * span <= 128))
    packed = (x_devices, y_devices, c_piece // members, group, members * span)

    def exchange(pieces):
        shape = pieces.shape
        pieces = pieces.reshape((x_devices * y_devices,) + packed[2:])
        return lax.all_to_all(pieces, ("gx",) + YZ, 0, 0, tiled=True).reshape(shape)

    def swap(pieces, count, shape):
        if paired:
            pairs = [[(d, d ^ k) for d in range(y_devices)] for k in range(y_devices)]
            pieces = [lax.ppermute(piece, YZ, pairs[k]) if k else piece for k, piece in enumerate(pieces)]
        else:
            pieces = jnp.stack(pieces).reshape(y_devices, -1, lanes)
            pieces = lax.all_to_all(pieces, YZ, 0, 0, tiled=True).reshape((count,) + shape)
        return [pieces[k].reshape(shape) for k in range(count)]

    def spectral(back, heads, weight, after=()):
        cells = (x_piece, c_piece, y_local, lanes)
        (part,) = small(y_down_body, [packed], y_mat, *swap(heads, y_devices, cells), after=after)
        part = exchange(part).reshape((x_devices, x_pieces, c_pieces) + packed[2:])
        kept, part = small(
            functools.partial(spectral_body, back), [(channels, span, j_local * modes), part.shape], part, x_mat, weight
        )
        part = exchange(part).reshape(packed)
        pieces = small(y_up_body, [cells] * y_devices, part, y_mat_t)
        return swap(pieces, blocks, block_head.shape), kept

    weight = jnp.transpose(spectral_weight, (2, 3, 1, 4, 0, 5)).reshape(channels, channels, span, j_local * modes)

    heads, after = [None] * blocks, ()
    half = -(-blocks // 2)
    for first, count in ((half, blocks - half), (0, half)):
        if count:
            heads[first : first + count] = head_call(first, count, after)
            after = (heads[first],)
    middle, modes_in = spectral(False, heads, weight, (weight, mix_up, mix_back))
    grads = ()
    for first, count in groups:
        grads, heads[first : first + count] = inner_call(first, count, middle, grads)
    middle, grad_modes = spectral(True, heads, weight)
    spec = whole(modes_in.shape)
    grad_spectral = call(
        outer_product_body, (j_local,), [spec, spec],
        pl.BlockSpec((1,) + spectral_weight.shape[1:], lambda j: (j, 0, 0, 0, 0, 0)),
        jax.ShapeDtypeStruct(spectral_weight.shape, jnp.float32),
        spectral_weight.size, 16 * spectral_weight.size, (modes_in, grad_modes),
    )
    field = ()
    for first, count in sorted(groups):
        field = outer_call(first, count, middle, grads, field)
    return field[0], grad_spectral


def solution(mesh):
    in_specs = (
        P("parts", None, "gx", YZ, None),
        P("parts", None, "gx", YZ, None),
        P(YZ, "gx", None, None, None, None),
        P(),
    )
    out_specs = (
        P("parts", None, "gx", YZ, None),
        P(("parts",) + YZ, "gx", None, None, None, None),
    )
    body = functools.partial(shards, mesh.shape["gx"], mesh.shape["gy"] * mesh.shape["gz"])
    return jax.shard_map(body, mesh=mesh, in_specs=in_specs, out_specs=out_specs, check_vma=False)
```

```python
import functools
import math

import jax
import jax.numpy as jnp
import ml_dtypes
import numpy as np
from jax import lax
from jax.experimental import pallas as pl
from jax.experimental.pallas import tpu as pltpu
from jax.sharding import PartitionSpec as P

YZ = ("gy", "gz")
HALF_ROOT = 1.0 / math.sqrt(2.0)
DENSITY = 1.0 / math.sqrt(2.0 * math.pi)


def basis(row_count, extent):
    row = np.arange(row_count)[:, None]
    cell = np.arange(extent)[None, :]
    radians = ((row + 1) // 2 * cell % extent) * (2.0 * math.pi / extent)
    wave = np.where(row % 2 == 0, np.cos(radians), np.sin(radians))
    scale = np.where(row == 0, math.sqrt(1.0 / extent), math.sqrt(2.0 / extent))
    return (wave * scale).astype(ml_dtypes.bfloat16).astype(np.float32)


def narrow(table):
    return np.asarray(table, dtype=ml_dtypes.bfloat16)


def dot(left, right, left_dim=1, right_dim=0):
    return lax.dot_general(
        left, right, (((left_dim,), (right_dim,)), ((), ())), preferred_element_type=jnp.float32
    )


def gelu_slope(value):
    size = jnp.abs(value)
    bell = jnp.exp2(value * value * (-0.5 * math.log2(math.e)))
    span = 1.0 + (0.3275911 * HALF_ROOT) * size
    t = pl.reciprocal(span, approx=True)
    t = t * (2.0 - span * t)
    tail = t * (
        0.5 * 0.254829592
        + t * (0.5 * -0.284496736 + t * (0.5 * 1.421413741 + t * (0.5 * -1.453152027 + t * (0.5 * 1.061405429))))
    )
    low = bell * (tail - DENSITY * size)
    return jnp.where(value >= 0.0, 1.0 - low, low)


ANY = pl.BlockSpec(memory_space=pl.ANY)


def call(body, grid, in_specs, out_specs, out_shape, args, order=None, scratch=(), aliases={}, after=()):
    lead = 0 if order is None else 1
    count = lead + len(args)

    def placed(*refs):
        body(*refs[:count], *refs[count + len(after) :])

    spec = pltpu.PrefetchScalarGridSpec(
        num_scalar_prefetch=lead,
        grid=grid,
        in_specs=list(in_specs) + [ANY] * len(after),
        out_specs=out_specs,
        scratch_shapes=scratch,
    )
    return pl.pallas_call(
        placed,
        grid_spec=spec,
        out_shape=out_shape,
        input_output_aliases={lead + operand: out for operand, out in aliases.items()},
        compiler_params=pltpu.CompilerParams(vmem_limit_bytes=52 * 1024 * 1024),
        cost_estimate=pl.CostEstimate(flops=0, bytes_accessed=0, transcendentals=0),
    )(*(() if order is None else (order,)), *args, *after)


def whole(shape):
    return pl.BlockSpec(shape, lambda *_: (0,) * len(shape))


def wide(ref, cell, times):
    channels, _, y_local, depth = ref.shape[1:]
    return jnp.concatenate([ref[t, :, cell].reshape(channels * y_local, depth) for t in times], axis=1)


def admit(held, pieces, sub):
    for e, piece in enumerate(pieces):

        @pl.when(pl.program_id(0) == e * sub)
        def _(piece=piece):
            held[...] = piece[...]


def release(held, pieces, sub):
    for e, piece in enumerate(pieces):

        @pl.when(pl.program_id(0) == e * sub + sub - 1)
        def _(piece=piece):
            piece[...] = held[...]


def own_cells(sub, cells):
    return pl.ds(lax.rem(pl.program_id(0), sub) * cells, cells)


def head_body(sub, order_ref, field_ref, table_ref, *refs):
    heads, held = refs[:-1], refs[-1]
    steps, _, cells, _, depth = field_ref.shape
    first = lax.rem(pl.program_id(0), sub) * cells
    for cell in range(cells):
        total = 0.0
        for t in range(0, steps, 2):
            total += dot(wide(field_ref, cell, (t, t + 1)), table_ref[t * depth : (t + 2) * depth, :])
        held[first + cell] = total.astype(jnp.bfloat16)
    release(held, heads, sub)


def inner_body(sub, count, order_ref, field_ref, cot_ref, mix_ref, syn_ref, table_ref, *refs):
    mids, (grad_ref, *heads), (mid_held, head_held) = refs[:count], refs[-count - 3 : -2], refs[-2:]
    steps, channels, cells, y_local, depth = field_ref.shape
    rows = channels * y_local
    band = math.gcd(rows, 32)
    admit(mid_held, mids, sub)
    middle = mid_held[own_cells(sub, cells)].reshape(cells * rows, -1)
    total = 0.0
    for t in range(0, steps, 2):
        lanes = slice(t * depth, (t + 2) * depth)
        spread = dot(middle, syn_ref[:, lanes])
        bands = []
        for cell in range(cells):
            preact = spread[cell * rows : (cell + 1) * rows] + dot(mix_ref[...], wide(field_ref, cell, (t, t + 1)))
            cot = wide(cot_ref, cell, (t, t + 1))
            for r in range(0, rows, band):
                slope = gelu_slope(preact[r : r + band])
                bands.append((cot[r : r + band].astype(jnp.float32) * slope).astype(jnp.bfloat16))
        grad = jnp.concatenate(bands, axis=0)
        for cell in range(cells):
            for k in range(2):
                part = grad[cell * rows : (cell + 1) * rows, k * depth : (k + 1) * depth]
                grad_ref[t + k, :, cell] = part.reshape(channels, y_local, depth)
        total += dot(grad, table_ref[lanes, :])
    head_held[own_cells(sub, cells)] = total.astype(jnp.bfloat16).reshape((cells,) + head_held.shape[1:])
    release(head_held, heads, sub)


def outer_body(sub, count, order_ref, grad_ref, mix_ref, syn_ref, *refs):
    mids, out_ref, mid_held = refs[:count], refs[-2], refs[-1]
    steps, channels, cells, y_local, depth = grad_ref.shape
    rows = channels * y_local
    admit(mid_held, mids, sub)
    middle = mid_held[own_cells(sub, cells)].reshape(cells * rows, -1)
    for t in range(0, steps, 2):
        spread = dot(middle, syn_ref[:, t * depth : (t + 2) * depth])
        for cell in range(cells):
            total = spread[cell * rows : (cell + 1) * rows] + dot(mix_ref[...], wide(grad_ref, cell, (t, t + 1)))
            total = total.astype(jnp.bfloat16)
            for k in range(2):
                out_ref[t + k, :, cell] = total[:, k * depth : (k + 1) * depth].reshape(channels, y_local, depth)


def y_down_body(table_ref, *refs):
    pieces, out_ref = refs[:-1], refs[-1]
    cells, channels = pieces[0].shape[:2]
    planes, owners, groups, height, width = out_ref.shape
    members = channels // groups
    span = width // members
    for k in range(groups):
        done = []
        for c in range(k * members, (k + 1) * members):
            stacked = jnp.concatenate([piece[x, c] for piece in pieces for x in range(cells)], axis=0)
            done.append(dot(table_ref[...], stacked).astype(jnp.bfloat16))
        for g in range(planes):
            piece = jnp.concatenate([part[:, g * span : (g + 1) * span] for part in done], axis=1)
            out_ref[g, :, k] = piece.reshape(owners, height, width)


def y_up_body(rows_ref, table_ref, *pieces):
    planes, owners, groups, _, width = rows_ref.shape
    cells, channels, y_local, _ = pieces[0].shape
    members = channels // groups
    span = width // members
    for c in range(channels):
        lanes = slice(c % members * span, (c % members + 1) * span)
        stacked = jnp.concatenate(
            [
                jnp.concatenate([rows_ref[g, s, c // members][:, lanes] for g in range(planes)], axis=1)
                for s in range(owners)
            ],
            axis=0,
        )
        done = dot(table_ref[...], stacked).astype(jnp.bfloat16)
        for k, piece in enumerate(pieces):
            for x in range(cells):
                start = (k * cells + x) * y_local
                piece[x, c] = done[start : start + y_local]


def spectral_body(back, rows_ref, table_ref, weight_ref, modes_ref, out_ref):
    planes, x_pieces, c_pieces, groups, height, width = rows_ref.shape
    channels, span, lanes = modes_ref.shape
    members = width // span
    for h in range(c_pieces):
        for k in range(groups):
            stacked = jnp.concatenate(
                [rows_ref[g, x, h, k] for g in range(planes) for x in range(x_pieces)], axis=0
            )
            first = (h * groups + k) * members
            done = dot(stacked, table_ref[...], 0, 0).astype(jnp.bfloat16)
            modes_ref[first : first + members] = done.reshape(members, span, lanes)
    held = weight_ref.shape[:1] + weight_ref.shape[3:]
    modes = [modes_ref[c].astype(jnp.float32).reshape(held) for c in range(channels)]
    for h in range(c_pieces):
        for k in range(groups):
            mixed = []
            for m in range(members):
                to = (h * groups + k) * members + m
                total = 0.0
                for of in range(channels):
                    weight = weight_ref[:, to, of] if back else weight_ref[:, of, to]
                    total += weight.astype(jnp.float32) * modes[of]
                mixed.append(total.reshape(span, lanes).astype(jnp.bfloat16))
            done = dot(table_ref[...], jnp.concatenate(mixed, axis=0), 1, 1).astype(jnp.bfloat16)
            for g in range(planes):
                for x in range(x_pieces):
                    start = (g * x_pieces + x) * height
                    out_ref[g, x, h, k] = done[start : start + height]


def weight_body(weight_ref, out_ref):
    out_ref[0] = jnp.concatenate([weight_ref[j, 0] for j in range(weight_ref.shape[0])], axis=-1)


def outer_product_body(left_ref, right_ref, out_ref):
    _, q_local, channels, _, time_modes, modes = out_ref.shape
    for j in range(left_ref.shape[2] // modes):

        @pl.when(pl.program_id(0) == j)
        def _(j=j):
            lanes = slice(j * modes, (j + 1) * modes)
            left = left_ref[:, :, lanes].astype(jnp.float32)
            right = right_ref[:, :, lanes].astype(jnp.float32)
            for q in range(q_local):
                rows = slice(q * time_modes, (q + 1) * time_modes)
                for c in range(channels):
                    out_ref[0, q, c] = left[c, rows] * right[:, rows]


def shards(x_devices, y_devices, state_field, cotangent, spectral_weight, point_weight):
    steps, channels, x_local, y_local, depth = state_field.shape
    j_local, q_local = spectral_weight.shape[:2]
    time_modes, modes = spectral_weight.shape[4:]
    lanes = time_modes * modes
    rows = channels * y_local
    x_extent, y_extent = x_local * x_devices, y_local * y_devices
    bf16 = jnp.bfloat16

    x_pieces = math.gcd(x_local, y_devices)
    c_pieces = y_devices // x_pieces
    x_piece, c_piece = x_local // x_pieces, channels // c_pieces
    group = x_piece * j_local

    paired = c_pieces == 1 and y_devices & (y_devices - 1) == 0
    blocks = x_pieces
    me = lax.axis_index(YZ)
    order = jnp.arange(blocks, dtype=jnp.int32) ^ (me.astype(jnp.int32) if paired else 0)

    time_table, depth_table = basis(time_modes, steps), basis(modes, depth)
    x_table, y_table = basis(modes, x_extent), basis(modes, y_extent)
    synth = np.einsum("pt,qz->qptz", time_table, depth_table).reshape(lanes, steps * depth)
    y_mat = np.einsum("xw,djsy->dxjswy", np.eye(x_piece), y_table.reshape(y_devices, j_local, y_devices, y_local))
    y_mat = y_mat.reshape(y_devices * group, y_devices, x_piece * y_local)
    seen = [[d ^ k if paired else k for k in range(y_devices)] for d in range(y_devices if paired else 1)]
    y_mats = np.stack([y_mat[:, owners].reshape(y_devices * group, -1) for owners in seen])
    mine = me if paired else 0
    x_mat = np.einsum("jk,ix->xjki", np.eye(j_local), x_table).reshape(x_extent * j_local, j_local * modes)
    syn, ana, x_mat = jnp.asarray(narrow(synth)), jnp.asarray(narrow(synth.T)), jnp.asarray(narrow(x_mat))
    y_mat = lax.dynamic_index_in_dim(jnp.asarray(narrow(y_mats)), mine, 0, keepdims=False)
    y_mat_t = lax.dynamic_index_in_dim(jnp.asarray(narrow(y_mats.swapaxes(1, 2))), mine, 0, keepdims=False)
    eye = jnp.eye(y_local, dtype=bf16)
    mix_up, mix_back = jnp.kron(point_weight.T, eye), jnp.kron(point_weight, eye)

    block_head = jax.ShapeDtypeStruct((x_piece, rows, lanes), bf16)
    full_field = jax.ShapeDtypeStruct(state_field.shape, bf16)
    held = pltpu.VMEM(block_head.shape, bf16)
    head_step, step = math.gcd(x_piece, 4), math.gcd(x_piece, 2)

    def grouped(first, step):
        sub = x_piece // step
        where = lambda g, order: (0, 0, order[first + g // sub] * sub + g % sub, 0, 0)
        return pl.BlockSpec((steps, channels, step, y_local, depth), where)

    pairs = [(k, min(2, blocks - k)) for k in range(0, blocks, 2)]
    groups = [(0, 1)] + pairs[1:] + [(1, 1)] if blocks > 1 else pairs

    def head_call(first, count, after):
        sub = x_piece // head_step
        return call(
            functools.partial(head_body, sub), (count * sub,), [grouped(first, head_step), whole(ana.shape)],
            [whole(block_head.shape)] * count, [block_head] * count,
            (state_field, ana), order, [held], after=after,
        )

    def inner_call(first, count, middle, grads, after):
        sub = x_piece // step
        tables = (mix_up, syn, ana)
        spec = grouped(first, step)
        done = call(
            functools.partial(inner_body, sub, count), (count * sub,),
            [spec] * 2 + [whole(arg.shape) for arg in tables] + [whole(block_head.shape)] * count + [ANY] * len(grads),
            [spec] + [whole(block_head.shape)] * count, [full_field] + [block_head] * count,
            (state_field, cotangent, *tables, *middle[first : first + count], *grads), order, [held, held],
            {5 + count: 0} if grads else {}, after,
        )
        return done[:1], done[1:]

    def outer_call(first, count, middle, grads, field):
        sub = x_piece // step
        tables = (mix_back, syn)
        spec = grouped(first, step)
        return call(
            functools.partial(outer_body, sub, count), (count * sub,),
            [spec] + [whole(arg.shape) for arg in tables] + [whole(block_head.shape)] * count + [ANY] * len(field),
            [spec], [full_field],
            (*grads, *tables, *middle[first : first + count], *field), order, [held],
            {3 + count: 0} if field else {},
        )

    def small(body, outs, *args, after=()):
        shapes = [jax.ShapeDtypeStruct(out, bf16) for out in outs]
        return call(
            body, (1,), [whole(arg.shape) for arg in args], [whole(out) for out in outs], shapes, args, after=after
        )

    span = q_local * time_modes
    members = max(m for m in range(1, c_piece + 1) if c_piece % m == 0 and (m == 1 or m * span <= 128))
    packed = (x_devices, y_devices, c_piece // members, group, members * span)

    def exchange(pieces):
        shape = pieces.shape
        pieces = pieces.reshape((x_devices * y_devices,) + packed[2:])
        return lax.all_to_all(pieces, ("gx",) + YZ, 0, 0, tiled=True).reshape(shape)

    def send(k, piece):
        if not (paired and k):
            return piece
        return lax.ppermute(piece, YZ, [(d, d ^ k) for d in range(y_devices)])

    def settle(pieces, count, shape):
        if not paired:
            pieces = jnp.stack(pieces).reshape(y_devices, -1, lanes)
            pieces = lax.all_to_all(pieces, YZ, 0, 0, tiled=True).reshape((count,) + shape)
        return [pieces[k].reshape(shape) for k in range(count)]

    cells = (x_piece, c_piece, y_local, lanes)

    def analyze(back, heads, weight, after):
        (part,) = small(y_down_body, [packed], y_mat, *settle(heads, y_devices, cells), after=after)
        part = exchange(part).reshape((x_devices, x_pieces, c_pieces) + packed[2:])
        kept, part = small(
            functools.partial(spectral_body, back), [(channels, span, j_local * modes), part.shape], part, x_mat, weight
        )
        return kept, exchange(part).reshape(packed)

    def synthesize(part, after):
        pieces = small(y_up_body, [cells] * y_devices, part, y_mat_t, after=after)
        pieces = [send(k, piece) for k, piece in enumerate(pieces)]
        return settle(pieces, blocks, block_head.shape)

    weight = call(
        weight_body, (q_local,),
        [pl.BlockSpec((j_local, 1, channels, channels, time_modes, modes), lambda q: (0, q, 0, 0, 0, 0))],
        pl.BlockSpec((1, channels, channels, time_modes, j_local * modes), lambda q: (q, 0, 0, 0, 0)),
        jax.ShapeDtypeStruct((q_local, channels, channels, time_modes, j_local * modes), bf16), (spectral_weight,),
    )

    heads, after = [None] * blocks, ()
    for first, count in ((6, 2), (2, 4), (0, 2)) if blocks == 8 else ((0, blocks),):
        done = head_call(first, count, after)
        heads[first : first + count] = [send(first + e, piece) for e, piece in enumerate(done)]
        after = (done[0],) if first == 6 else tuple(heads[6:])
    modes_in, part = analyze(False, heads, weight, (weight, mix_up, mix_back, y_mat_t))
    middle = synthesize(part, ())

    grads, sent = (), [(), ()]
    for first, count in groups:
        grads, done = inner_call(first, count, middle, grads, sent[-2])
        heads[first : first + count] = [send(first + e, piece) for e, piece in enumerate(done)]
        sent.append(tuple(heads[max(first, 1) : first + count]) if paired else ())
    grad_modes, part = analyze(True, heads, weight, ())
    spec = whole(modes_in.shape)
    grad_spectral = call(
        outer_product_body, (j_local,), [spec, spec],
        pl.BlockSpec((1,) + spectral_weight.shape[1:], lambda j: (j, 0, 0, 0, 0, 0)),
        jax.ShapeDtypeStruct(spectral_weight.shape, jnp.float32),
        (modes_in, grad_modes),
    )
    middle = synthesize(part, (grad_spectral,))
    field = ()
    for first, count in pairs:
        field = outer_call(first, count, middle, grads, field)
    return field[0], grad_spectral


def solution(mesh):
    in_specs = (
        P("parts", None, "gx", YZ, None),
        P("parts", None, "gx", YZ, None),
        P(YZ, "gx", None, None, None, None),
        P(),
    )
    out_specs = (
        P("parts", None, "gx", YZ, None),
        P(("parts",) + YZ, "gx", None, None, None, None),
    )
    body = functools.partial(shards, mesh.shape["gx"], mesh.shape["gy"] * mesh.shape["gz"])
    return jax.shard_map(body, mesh=mesh, in_specs=in_specs, out_specs=out_specs, check_vma=False)
```

```python
import functools
import math

import jax
import jax.numpy as jnp
import ml_dtypes
import numpy as np
from jax import lax
from jax.experimental import pallas as pl
from jax.experimental.pallas import tpu as pltpu
from jax.sharding import PartitionSpec as P

YZ = ("gy", "gz")
HALF_ROOT = 1.0 / math.sqrt(2.0)
DENSITY = 1.0 / math.sqrt(2.0 * math.pi)


def basis(row_count, extent):
    row = np.arange(row_count)[:, None]
    cell = np.arange(extent)[None, :]
    radians = ((row + 1) // 2 * cell % extent) * (2.0 * math.pi / extent)
    wave = np.where(row % 2 == 0, np.cos(radians), np.sin(radians))
    scale = np.where(row == 0, math.sqrt(1.0 / extent), math.sqrt(2.0 / extent))
    return (wave * scale).astype(ml_dtypes.bfloat16).astype(np.float32)


def narrow(table):
    return np.asarray(table, dtype=ml_dtypes.bfloat16)


def dot(left, right, left_dim=1, right_dim=0):
    return lax.dot_general(
        left, right, (((left_dim,), (right_dim,)), ((), ())), preferred_element_type=jnp.float32
    )


def gelu_slope(value):
    size = jnp.abs(value)
    bell = jnp.exp2(value * value * (-0.5 * math.log2(math.e)))
    span = 1.0 + (0.3275911 * HALF_ROOT) * size
    t = pl.reciprocal(span, approx=True)
    t = t * (2.0 - span * t)
    tail = t * (
        0.5 * 0.254829592
        + t * (0.5 * -0.284496736 + t * (0.5 * 1.421413741 + t * (0.5 * -1.453152027 + t * (0.5 * 1.061405429))))
    )
    low = bell * (tail - DENSITY * size)
    return jnp.where(value >= 0.0, 1.0 - low, low)


ANY = pl.BlockSpec(memory_space=pl.ANY)


def call(body, grid, in_specs, out_specs, out_shape, args, order=None, scratch=(), aliases={}, after=(), carry=()):
    lead = 0 if order is None else 1
    count, outs = lead + len(args), len(out_shape)
    idle = len(after) + len(carry)

    def placed(*refs):
        ends = count + idle, count + idle + outs, count + idle + outs + len(carry)
        body(*refs[:count], *refs[ends[0] : ends[1]], *refs[ends[2] :])

    spec = pltpu.PrefetchScalarGridSpec(
        num_scalar_prefetch=lead,
        grid=grid,
        in_specs=list(in_specs) + [ANY] * idle,
        out_specs=list(out_specs) + [ANY] * len(carry),
        scratch_shapes=scratch,
    )
    kept = {count + len(after) + e: outs + e for e in range(len(carry))}
    return pl.pallas_call(
        placed,
        grid_spec=spec,
        out_shape=list(out_shape) + [jax.ShapeDtypeStruct(x.shape, x.dtype) for x in carry],
        input_output_aliases={lead + operand: out for operand, out in aliases.items()} | kept,
        compiler_params=pltpu.CompilerParams(vmem_limit_bytes=50 * 1024 * 1024),
        cost_estimate=pl.CostEstimate(flops=0, bytes_accessed=0, transcendentals=0),
    )(*(() if order is None else (order,)), *args, *after, *carry)


def whole(shape):
    return pl.BlockSpec(shape, lambda *_: (0,) * len(shape))


def wide(ref, cell, times):
    channels, _, y_local, depth = ref.shape[1:]
    return jnp.concatenate([ref[t, :, cell].reshape(channels * y_local, depth) for t in times], axis=1)


def pieces_of(order_ref, first, unit, pieces, held):
    cells = held.shape[0] // unit
    for e, piece in enumerate(pieces):
        start = lax.rem(order_ref[first + e], unit) * cells
        yield e // unit, pl.ds(start, cells), piece


def admit(order_ref, first, unit, pieces, held):
    for which, cells, piece in pieces_of(order_ref, first, unit, pieces, held):

        @pl.when((pl.program_id(0) == which) & (pl.program_id(1) == 0))
        def _(cells=cells, piece=piece):
            held[cells] = piece[...]


def release(order_ref, first, unit, pieces, held):
    for which, cells, piece in pieces_of(order_ref, first, unit, pieces, held):

        @pl.when((pl.program_id(0) == which) & (pl.program_id(1) == pl.num_programs(1) - 1))
        def _(cells=cells, piece=piece):
            piece[...] = held[cells].astype(piece.dtype)


def add_time(held, cells, part):
    before = jnp.where(pl.program_id(1) == 0, 0.0, held[cells])
    held[cells] = before + part.reshape(before.shape)


def bunches(cells, most):
    size = math.gcd(cells, most)
    return [slice(c, c + size) for c in range(0, cells, size)]


def head_body(first, unit, order_ref, field_ref, table_ref, *refs):
    heads, held = refs[:-1], refs[-1]
    times = range(field_ref.shape[0])
    for cells in bunches(field_ref.shape[2], 4):
        values = jnp.concatenate([wide(field_ref, cell, times) for cell in range(cells.start, cells.stop)], axis=0)
        add_time(held, cells, dot(values, table_ref[...]))
    release(order_ref, first, unit, heads, held)


def inner_body(first, unit, count, order_ref, field_ref, cot_ref, mix_ref, syn_ref, table_ref, *refs):
    mids, (grad_ref, *heads), (mid_held, head_held) = refs[:count], refs[-count - 3 : -2], refs[-2:]
    span, channels, _, y_local, depth = field_ref.shape
    rows = channels * y_local
    band = math.gcd(rows, 32)
    admit(order_ref, first, unit, mids, mid_held)
    for cells in bunches(field_ref.shape[2], 2):
        middle = mid_held[cells]
        spread = dot(middle.reshape(-1, middle.shape[2]), syn_ref[...])
        grads = []
        for k, cell in enumerate(range(cells.start, cells.stop)):
            values = wide(field_ref, cell, range(span))
            preact = spread[k * rows : (k + 1) * rows] + dot(mix_ref[...], values)
            cot = wide(cot_ref, cell, range(span))
            bands = []
            for r in range(0, rows, band):
                slope = gelu_slope(preact[r : r + band])
                bands.append((cot[r : r + band].astype(jnp.float32) * slope).astype(jnp.bfloat16))
            grads.append(jnp.concatenate(bands, axis=0))
            for t in range(span):
                part = grads[-1][:, t * depth : (t + 1) * depth]
                grad_ref[t, :, cell] = part.reshape(channels, y_local, depth)
        add_time(head_held, cells, dot(jnp.concatenate(grads, axis=0), table_ref[...]))
    release(order_ref, first, unit, heads, head_held)


def outer_body(first, unit, count, order_ref, grad_ref, mix_ref, syn_ref, *refs):
    mids, out_ref, mid_held = refs[:count], refs[-2], refs[-1]
    span, channels, _, y_local, depth = grad_ref.shape
    rows = channels * y_local
    admit(order_ref, first, unit, mids, mid_held)
    for cells in bunches(grad_ref.shape[2], 2):
        middle = mid_held[cells]
        spread = dot(middle.reshape(-1, middle.shape[2]), syn_ref[...])
        for k, cell in enumerate(range(cells.start, cells.stop)):
            total = spread[k * rows : (k + 1) * rows] + dot(mix_ref[...], wide(grad_ref, cell, range(span)))
            total = total.astype(jnp.bfloat16)
            for t in range(span):
                out_ref[t, :, cell] = total[:, t * depth : (t + 1) * depth].reshape(channels, y_local, depth)


def y_down_body(table_ref, *refs):
    pieces, out_ref = refs[:-1], refs[-1]
    cells, channels = pieces[0].shape[:2]
    planes, owners, groups, height, width = out_ref.shape
    members = channels // groups
    span = width // members
    for k in range(groups):
        done = []
        for c in range(k * members, (k + 1) * members):
            stacked = jnp.concatenate([piece[x, c] for piece in pieces for x in range(cells)], axis=0)
            done.append(dot(table_ref[...], stacked).astype(jnp.bfloat16))
        for g in range(planes):
            piece = jnp.concatenate([part[:, g * span : (g + 1) * span] for part in done], axis=1)
            out_ref[g, :, k] = piece.reshape(owners, height, width)


def y_up_body(rows_ref, table_ref, *pieces):
    planes, owners, groups, _, width = rows_ref.shape
    cells, channels, y_local, _ = pieces[0].shape
    members = channels // groups
    span = width // members
    for c in range(channels):
        lanes = slice(c % members * span, (c % members + 1) * span)
        stacked = jnp.concatenate(
            [
                jnp.concatenate([rows_ref[g, s, c // members][:, lanes] for g in range(planes)], axis=1)
                for s in range(owners)
            ],
            axis=0,
        )
        done = dot(table_ref[...], stacked).astype(jnp.bfloat16)
        for k, piece in enumerate(pieces):
            for x in range(cells):
                start = (k * cells + x) * y_local
                piece[x, c] = done[start : start + y_local]


def spectral_body(back, rows_ref, table_ref, weight_ref, modes_ref, out_ref):
    planes, x_pieces, c_pieces, groups, height, width = rows_ref.shape
    channels, span, lanes = modes_ref.shape
    members = width // span
    for h in range(c_pieces):
        for k in range(groups):
            stacked = jnp.concatenate(
                [rows_ref[g, x, h, k] for g in range(planes) for x in range(x_pieces)], axis=0
            )
            first = (h * groups + k) * members
            done = dot(stacked, table_ref[...], 0, 0).astype(jnp.bfloat16)
            modes_ref[first : first + members] = done.reshape(members, span, lanes)
    for h in range(c_pieces):
        for k in range(groups):
            mixed = []
            for m in range(members):
                to = (h * groups + k) * members + m
                total = 0.0
                for of in range(channels):
                    weight = weight_ref[to, of] if back else weight_ref[of, to]
                    total += weight.astype(jnp.float32) * modes_ref[of].astype(jnp.float32)
                mixed.append(total.astype(jnp.bfloat16))
            done = dot(table_ref[...], jnp.concatenate(mixed, axis=0), 1, 1).astype(jnp.bfloat16)
            for g in range(planes):
                for x in range(x_pieces):
                    start = (g * x_pieces + x) * height
                    out_ref[g, x, h, k] = done[start : start + height]


def weight_body(weight_ref, out_ref):
    j_local, q_local, _, channels = weight_ref.shape[:4]
    for o in range(channels):
        rows = [
            jnp.concatenate([weight_ref[j, q, 0, o].astype(jnp.float32) for j in range(j_local)], axis=1)
            for q in range(q_local)
        ]
        out_ref[0, o] = jnp.concatenate(rows, axis=0).astype(out_ref.dtype)


def outer_product_body(left_ref, right_ref, out_ref):
    _, q_local, channels, _, time_modes, modes = out_ref.shape
    for j in range(left_ref.shape[2] // modes):

        @pl.when(pl.program_id(0) == j)
        def _(j=j):
            lanes = slice(j * modes, (j + 1) * modes)
            left = left_ref[:, :, lanes].astype(jnp.float32)
            right = right_ref[:, :, lanes].astype(jnp.float32)
            for q in range(q_local):
                rows = slice(q * time_modes, (q + 1) * time_modes)
                for c in range(channels):
                    out_ref[0, q, c] = left[c, rows] * right[:, rows]


def shards(x_devices, y_devices, state_field, cotangent, spectral_weight, point_weight):
    steps, channels, x_local, y_local, depth = state_field.shape
    j_local, q_local = spectral_weight.shape[:2]
    time_modes, modes = spectral_weight.shape[4:]
    lanes = time_modes * modes
    rows = channels * y_local
    x_extent, y_extent = x_local * x_devices, y_local * y_devices
    bf16 = jnp.bfloat16

    x_pieces = math.gcd(x_local, y_devices)
    c_pieces = y_devices // x_pieces
    x_piece, c_piece = x_local // x_pieces, channels // c_pieces
    group = x_piece * j_local

    paired = c_pieces == 1 and y_devices & (y_devices - 1) == 0
    blocks = x_pieces
    me = lax.axis_index(YZ)
    order = jnp.arange(blocks, dtype=jnp.int32) ^ (me.astype(jnp.int32) if paired else 0)

    time_table, depth_table = basis(time_modes, steps), basis(modes, depth)
    x_table, y_table = basis(modes, x_extent), basis(modes, y_extent)
    synth = np.einsum("pt,qz->qptz", time_table, depth_table).reshape(lanes, steps * depth)
    y_mat = np.einsum("xw,djsy->dxjswy", np.eye(x_piece), y_table.reshape(y_devices, j_local, y_devices, y_local))
    y_mat = y_mat.reshape(y_devices * group, y_devices, x_piece * y_local)
    seen = [[d ^ k if paired else k for k in range(y_devices)] for d in range(y_devices if paired else 1)]
    y_mats = np.stack([y_mat[:, owners].reshape(y_devices * group, -1) for owners in seen])
    mine = me if paired else 0
    x_mat = np.einsum("jk,ix->xjki", np.eye(j_local), x_table).reshape(x_extent * j_local, j_local * modes)
    syn, ana, x_mat = jnp.asarray(narrow(synth)), jnp.asarray(narrow(synth.T)), jnp.asarray(narrow(x_mat))
    y_mat = lax.dynamic_index_in_dim(jnp.asarray(narrow(y_mats)), mine, 0, keepdims=False)
    y_mat_t = lax.dynamic_index_in_dim(jnp.asarray(narrow(y_mats.swapaxes(1, 2))), mine, 0, keepdims=False)
    eye = jnp.eye(y_local, dtype=bf16)
    mix_up, mix_back = jnp.kron(point_weight.T, eye), jnp.kron(point_weight, eye)

    block_head = jax.ShapeDtypeStruct((x_piece, rows, lanes), bf16)
    full_field = jax.ShapeDtypeStruct(state_field.shape, bf16)
    span_t = math.gcd(steps, 2)

    def plan(first, unit, count):
        where = lambda n, t, order: (t, 0, lax.div(order[first + n * unit], unit), 0, 0)
        field = pl.BlockSpec((span_t, channels, unit * x_piece, y_local, depth), where)
        syn_spec = pl.BlockSpec((lanes, span_t * depth), lambda n, t, order: (0, t))
        ana_spec = pl.BlockSpec((span_t * depth, lanes), lambda n, t, order: (t, 0))
        held = (unit * x_piece, rows, lanes)
        return (count // unit, steps // span_t), field, syn_spec, ana_spec, held

    pairs = [(k, min(2, blocks - k)) for k in range(0, blocks, 2)]
    groups = [(1, 1)] + pairs[1:] + [(0, 1)] if blocks > 1 else pairs

    def head_call(first, unit, count, after):
        grid, field, _, ana_spec, held = plan(first, unit, count)
        return call(
            functools.partial(head_body, first, unit), grid, [field, ana_spec],
            [whole(block_head.shape)] * count, [block_head] * count, (state_field, ana), order,
            [pltpu.VMEM(held, jnp.float32)], after=after,
        )

    def inner_call(first, count, middle, grads, after, carry):
        grid, field, syn_spec, ana_spec, held = plan(first, count, count)
        done = call(
            functools.partial(inner_body, first, count, count), grid,
            [field] * 2 + [whole(mix_up.shape), syn_spec, ana_spec] + [whole(block_head.shape)] * count + [ANY] * len(grads),
            [field] + [whole(block_head.shape)] * count, [full_field] + [block_head] * count,
            (state_field, cotangent, mix_up, syn, ana, *middle[first : first + count], *grads), order,
            [pltpu.VMEM(held, bf16), pltpu.VMEM(held, jnp.float32)], {5 + count: 0} if grads else {}, after, carry,
        )
        return done[:1], done[1 : 1 + count], done[1 + count :]

    def outer_call(first, count, middle, grads, field, carry):
        grid, spec, syn_spec, _, held = plan(first, count, count)
        done = call(
            functools.partial(outer_body, first, count, count), grid,
            [spec, whole(mix_back.shape), syn_spec] + [whole(block_head.shape)] * count + [ANY] * len(field),
            [spec], [full_field], (*grads, mix_back, syn, *middle[first : first + count], *field), order,
            [pltpu.VMEM(held, bf16)], {3 + count: 0} if field else {}, (), carry,
        )
        return done[:1], done[1:]

    def small(body, outs, *args, after=()):
        shapes = [jax.ShapeDtypeStruct(out, bf16) for out in outs]
        return call(
            body, (1,), [whole(arg.shape) for arg in args], [whole(out) for out in outs], shapes, args, after=after
        )

    span = q_local * time_modes
    members = max(m for m in range(1, c_piece + 1) if c_piece % m == 0 and (m == 1 or m * span <= 128))
    packed = (x_devices, y_devices, c_piece // members, group, members * span)

    def exchange(pieces):
        shape = pieces.shape
        pieces = pieces.reshape((x_devices * y_devices,) + packed[2:])
        return lax.all_to_all(pieces, ("gx",) + YZ, 0, 0, tiled=True).reshape(shape)

    def send(k, piece):
        if not (paired and k):
            return piece
        return lax.ppermute(piece, YZ, [(d, d ^ k) for d in range(y_devices)])

    def settle(pieces, count, shape):
        if not paired:
            pieces = jnp.stack(pieces).reshape(y_devices, -1, lanes)
            pieces = lax.all_to_all(pieces, YZ, 0, 0, tiled=True).reshape((count,) + shape)
        return [pieces[k].reshape(shape) for k in range(count)]

    cells = (x_piece, c_piece, y_local, lanes)

    def analyze(heads):
        return small(y_down_body, [packed], y_mat, *settle(heads, y_devices, cells))[0]

    def mix(back, part, weight, after):
        part = exchange(part).reshape((x_devices, x_pieces, c_pieces) + packed[2:])
        kept, part = small(
            functools.partial(spectral_body, back), [(channels, span, j_local * modes), part.shape],
            part, x_mat, weight, after=after,
        )
        return kept, exchange(part).reshape(packed)

    def synthesize(part, after):
        pieces = small(y_up_body, [cells] * y_devices, part, y_mat_t, after=after)
        if paired:
            pieces = [piece.reshape(block_head.shape) for piece in pieces]
        late = pieces[6:] if paired else []
        return [send(k, piece) for k, piece in enumerate(pieces[: len(pieces) - len(late)])], late

    def rest(pieces, late):
        pieces = pieces + [send(len(pieces) + e, piece) for e, piece in enumerate(late)]
        return settle(pieces, blocks, block_head.shape)

    heads, after = [None] * blocks, ()
    for first, count in ((6, 2), (2, 4), (0, 2)) if blocks == 8 else ((0, blocks),):
        done = head_call(first, math.gcd(count, 2), count, after)
        heads[first : first + count] = [send(first + e, piece) for e, piece in enumerate(done)]
        after = (done[0],) if first == 6 else tuple(heads[6:])
    part = analyze(heads)
    (weight,) = call(
        weight_body, (channels,),
        [pl.BlockSpec((j_local, q_local, 1, channels, time_modes, modes), lambda c: (0, 0, c, 0, 0, 0))],
        [pl.BlockSpec((1, channels, span, j_local * modes), lambda c: (c, 0, 0, 0))],
        [jax.ShapeDtypeStruct((channels, channels, span, j_local * modes), bf16)], (spectral_weight,), after=(part,),
    )
    modes_in, part = mix(False, part, weight, (mix_up, mix_back, y_mat_t))

    middle, late = synthesize(part, ())
    sent, grads = [(), ()], ()
    if not paired:
        middle = rest(middle, late)
    for first, count in groups:
        grads, done, late = inner_call(first, count, middle, grads, sent[-2], late)
        if late:
            middle, late = rest(middle, late), []
        heads[first : first + count] = [send(first + e, piece) for e, piece in enumerate(done)]
        sent.append(tuple(heads[max(first, 1) : first + count]) if paired else ())
    part = analyze(heads)
    grad_modes, part = mix(True, part, weight, ())
    spec = whole(modes_in.shape)
    (grad_spectral,) = call(
        outer_product_body, (j_local,), [spec, spec],
        [pl.BlockSpec((1,) + spectral_weight.shape[1:], lambda j: (j, 0, 0, 0, 0, 0))],
        [jax.ShapeDtypeStruct(spectral_weight.shape, jnp.float32)], (modes_in, grad_modes),
    )
    middle, late = synthesize(part, (grad_spectral,))
    if not paired:
        middle = rest(middle, late)
    field = ()
    for first, count in pairs:
        field, late = outer_call(first, count, middle, grads, field, late)
        if late:
            middle, late = rest(middle, late), []
    return field[0], grad_spectral


def solution(mesh):
    in_specs = (
        P("parts", None, "gx", YZ, None),
        P("parts", None, "gx", YZ, None),
        P(YZ, "gx", None, None, None, None),
        P(),
    )
    out_specs = (
        P("parts", None, "gx", YZ, None),
        P(("parts",) + YZ, "gx", None, None, None, None),
    )
    body = functools.partial(shards, mesh.shape["gx"], mesh.shape["gy"] * mesh.shape["gz"])
    return jax.shard_map(body, mesh=mesh, in_specs=in_specs, out_specs=out_specs, check_vma=False)
```

```python
import functools
import math

import jax
import jax.numpy as jnp
import ml_dtypes
import numpy as np
from jax import lax
from jax.experimental import pallas as pl
from jax.experimental.pallas import tpu as pltpu
from jax.sharding import PartitionSpec as P

YZ = ("gy", "gz")
HALF_ROOT = 1.0 / math.sqrt(2.0)
DENSITY = 1.0 / math.sqrt(2.0 * math.pi)


def basis(row_count, extent):
    row = np.arange(row_count)[:, None]
    cell = np.arange(extent)[None, :]
    radians = ((row + 1) // 2 * cell % extent) * (2.0 * math.pi / extent)
    wave = np.where(row % 2 == 0, np.cos(radians), np.sin(radians))
    scale = np.where(row == 0, math.sqrt(1.0 / extent), math.sqrt(2.0 / extent))
    return (wave * scale).astype(ml_dtypes.bfloat16).astype(np.float32)


def narrow(table):
    return np.asarray(table, dtype=ml_dtypes.bfloat16)


def dot(left, right, left_dim=1, right_dim=0):
    return lax.dot_general(
        left, right, (((left_dim,), (right_dim,)), ((), ())), preferred_element_type=jnp.float32
    )


def gelu_slope(value):
    size = jnp.abs(value)
    bell = jnp.exp2(value * value * (-0.5 * math.log2(math.e)))
    span = 1.0 + (0.3275911 * HALF_ROOT) * size
    t = pl.reciprocal(span, approx=True)
    t = t * (2.0 - span * t)
    tail = t * (
        0.5 * 0.254829592
        + t * (0.5 * -0.284496736 + t * (0.5 * 1.421413741 + t * (0.5 * -1.453152027 + t * (0.5 * 1.061405429))))
    )
    low = bell * (tail - DENSITY * size)
    return jnp.where(value >= 0.0, 1.0 - low, low)


ANY = pl.BlockSpec(memory_space=pl.ANY)


def call(body, grid, in_specs, out_specs, out_shape, args, order=None, scratch=(), aliases={}, after=(), carry=()):
    lead = 0 if order is None else 1
    count, outs = lead + len(args), len(out_shape)
    idle = len(after) + len(carry)

    def placed(*refs):
        ends = count + idle, count + idle + outs, count + idle + outs + len(carry)
        body(*refs[:count], *refs[ends[0] : ends[1]], *refs[ends[2] :])

    spec = pltpu.PrefetchScalarGridSpec(
        num_scalar_prefetch=lead,
        grid=grid,
        in_specs=list(in_specs) + [ANY] * idle,
        out_specs=list(out_specs) + [ANY] * len(carry),
        scratch_shapes=scratch,
    )
    kept = {count + len(after) + e: outs + e for e in range(len(carry))}
    return pl.pallas_call(
        placed,
        grid_spec=spec,
        out_shape=list(out_shape) + [jax.ShapeDtypeStruct(x.shape, x.dtype) for x in carry],
        input_output_aliases={lead + operand: out for operand, out in aliases.items()} | kept,
        compiler_params=pltpu.CompilerParams(vmem_limit_bytes=50 * 1024 * 1024),
        cost_estimate=pl.CostEstimate(flops=0, bytes_accessed=0, transcendentals=0),
    )(*(() if order is None else (order,)), *args, *after, *carry)


def whole(shape):
    return pl.BlockSpec(shape, lambda *_: (0,) * len(shape))


def wide(ref, cell, times):
    channels, _, y_local, depth = ref.shape[1:]
    return jnp.concatenate([ref[t, :, cell].reshape(channels * y_local, depth) for t in times], axis=1)


def admit(held, pieces, sub):
    for e, piece in enumerate(pieces):

        @pl.when(pl.program_id(0) == e * sub)
        def _(piece=piece):
            held[...] = piece[...]


def release(held, pieces, sub):
    for e, piece in enumerate(pieces):

        @pl.when(pl.program_id(0) == e * sub + sub - 1)
        def _(piece=piece):
            piece[...] = held[...]


def own_cells(sub, cells):
    return pl.ds(lax.rem(pl.program_id(0), sub) * cells, cells)


def head_body(sub, order_ref, field_ref, table_ref, *refs):
    heads, held = refs[:-1], refs[-1]
    steps, _, cells, _, depth = field_ref.shape
    first = lax.rem(pl.program_id(0), sub) * cells
    for cell in range(cells):
        total = 0.0
        for t in range(0, steps, 2):
            total += dot(wide(field_ref, cell, (t, t + 1)), table_ref[t * depth : (t + 2) * depth, :])
        held[first + cell] = total.astype(jnp.bfloat16)
    release(held, heads, sub)


def inner_body(sub, count, order_ref, field_ref, cot_ref, mix_ref, syn_ref, table_ref, *refs):
    mids, (grad_ref, *heads), (mid_held, head_held) = refs[:count], refs[-count - 3 : -2], refs[-2:]
    steps, channels, cells, y_local, depth = field_ref.shape
    rows = channels * y_local
    band = math.gcd(rows, 32)
    admit(mid_held, mids, sub)
    middle = mid_held[own_cells(sub, cells)].reshape(cells * rows, -1)
    total = 0.0
    for t in range(0, steps, 2):
        lanes = slice(t * depth, (t + 2) * depth)
        spread = dot(middle, syn_ref[:, lanes])
        bands = []
        for cell in range(cells):
            preact = spread[cell * rows : (cell + 1) * rows] + dot(mix_ref[...], wide(field_ref, cell, (t, t + 1)))
            cot = wide(cot_ref, cell, (t, t + 1))
            for r in range(0, rows, band):
                slope = gelu_slope(preact[r : r + band])
                bands.append((cot[r : r + band].astype(jnp.float32) * slope).astype(jnp.bfloat16))
        grad = jnp.concatenate(bands, axis=0)
        for cell in range(cells):
            for k in range(2):
                part = grad[cell * rows : (cell + 1) * rows, k * depth : (k + 1) * depth]
                grad_ref[t + k, :, cell] = part.reshape(channels, y_local, depth)
        total += dot(grad, table_ref[lanes, :])
    head_held[own_cells(sub, cells)] = total.astype(jnp.bfloat16).reshape((cells,) + head_held.shape[1:])
    release(head_held, heads, sub)


def outer_body(sub, count, order_ref, grad_ref, mix_ref, syn_ref, *refs):
    mids, out_ref, mid_held = refs[:count], refs[-2], refs[-1]
    steps, channels, cells, y_local, depth = grad_ref.shape
    rows = channels * y_local
    admit(mid_held, mids, sub)
    middle = mid_held[own_cells(sub, cells)].reshape(cells * rows, -1)
    for t in range(0, steps, 2):
        spread = dot(middle, syn_ref[:, t * depth : (t + 2) * depth])
        for cell in range(cells):
            total = spread[cell * rows : (cell + 1) * rows] + dot(mix_ref[...], wide(grad_ref, cell, (t, t + 1)))
            total = total.astype(jnp.bfloat16)
            for k in range(2):
                out_ref[t + k, :, cell] = total[:, k * depth : (k + 1) * depth].reshape(channels, y_local, depth)


def y_down_body(table_ref, *refs):
    pieces, out_ref = refs[:-1], refs[-1]
    cells, channels = pieces[0].shape[:2]
    planes, owners, groups, height, width = out_ref.shape
    members = channels // groups
    span = width // members
    for k in range(groups):
        done = []
        for c in range(k * members, (k + 1) * members):
            stacked = jnp.concatenate([piece[x, c] for piece in pieces for x in range(cells)], axis=0)
            done.append(dot(table_ref[...], stacked).astype(jnp.bfloat16))
        for g in range(planes):
            piece = jnp.concatenate([part[:, g * span : (g + 1) * span] for part in done], axis=1)
            out_ref[g, :, k] = piece.reshape(owners, height, width)


def y_up_body(rows_ref, table_ref, *pieces):
    planes, owners, groups, _, width = rows_ref.shape
    cells, channels, y_local, _ = pieces[0].shape
    members = channels // groups
    span = width // members
    for c in range(channels):
        lanes = slice(c % members * span, (c % members + 1) * span)
        stacked = jnp.concatenate(
            [
                jnp.concatenate([rows_ref[g, s, c // members][:, lanes] for g in range(planes)], axis=1)
                for s in range(owners)
            ],
            axis=0,
        )
        done = dot(table_ref[...], stacked).astype(jnp.bfloat16)
        for k, piece in enumerate(pieces):
            for x in range(cells):
                start = (k * cells + x) * y_local
                piece[x, c] = done[start : start + y_local]


def spectral_body(back, rows_ref, table_ref, weight_ref, modes_ref, out_ref):
    planes, x_pieces, c_pieces, groups, height, width = rows_ref.shape
    channels, span, lanes = modes_ref.shape
    members = width // span
    for h in range(c_pieces):
        for k in range(groups):
            stacked = jnp.concatenate(
                [rows_ref[g, x, h, k] for g in range(planes) for x in range(x_pieces)], axis=0
            )
            first = (h * groups + k) * members
            done = dot(stacked, table_ref[...], 0, 0).astype(jnp.bfloat16)
            modes_ref[first : first + members] = done.reshape(members, span, lanes)
    for h in range(c_pieces):
        for k in range(groups):
            mixed = []
            for m in range(members):
                to = (h * groups + k) * members + m
                total = 0.0
                for of in range(channels):
                    weight = weight_ref[to, of] if back else weight_ref[of, to]
                    total += weight.astype(jnp.float32) * modes_ref[of].astype(jnp.float32)
                mixed.append(total.astype(jnp.bfloat16))
            done = dot(table_ref[...], jnp.concatenate(mixed, axis=0), 1, 1).astype(jnp.bfloat16)
            for g in range(planes):
                for x in range(x_pieces):
                    start = (g * x_pieces + x) * height
                    out_ref[g, x, h, k] = done[start : start + height]


def weight_body(weight_ref, out_ref):
    j_local, q_local, _, channels = weight_ref.shape[:4]
    for o in range(channels):
        rows = [
            jnp.concatenate([weight_ref[j, q, 0, o].astype(jnp.float32) for j in range(j_local)], axis=1)
            for q in range(q_local)
        ]
        out_ref[0, o] = jnp.concatenate(rows, axis=0).astype(out_ref.dtype)


def outer_product_body(left_ref, right_ref, out_ref):
    _, q_local, channels, _, time_modes, modes = out_ref.shape
    for j in range(left_ref.shape[2] // modes):

        @pl.when(pl.program_id(0) == j)
        def _(j=j):
            lanes = slice(j * modes, (j + 1) * modes)
            left = left_ref[:, :, lanes].astype(jnp.float32)
            right = right_ref[:, :, lanes].astype(jnp.float32)
            for q in range(q_local):
                rows = slice(q * time_modes, (q + 1) * time_modes)
                for c in range(channels):
                    out_ref[0, q, c] = left[c, rows] * right[:, rows]


def shards(x_devices, y_devices, state_field, cotangent, spectral_weight, point_weight):
    steps, channels, x_local, y_local, depth = state_field.shape
    j_local, q_local = spectral_weight.shape[:2]
    time_modes, modes = spectral_weight.shape[4:]
    lanes = time_modes * modes
    rows = channels * y_local
    x_extent, y_extent = x_local * x_devices, y_local * y_devices
    bf16 = jnp.bfloat16

    x_pieces = math.gcd(x_local, y_devices)
    c_pieces = y_devices // x_pieces
    x_piece, c_piece = x_local // x_pieces, channels // c_pieces
    group = x_piece * j_local

    paired = c_pieces == 1 and y_devices & (y_devices - 1) == 0
    blocks = x_pieces
    me = lax.axis_index(YZ)
    order = jnp.arange(blocks, dtype=jnp.int32) ^ (me.astype(jnp.int32) if paired else 0)

    time_table, depth_table = basis(time_modes, steps), basis(modes, depth)
    x_table, y_table = basis(modes, x_extent), basis(modes, y_extent)
    synth = np.einsum("pt,qz->qptz", time_table, depth_table).reshape(lanes, steps * depth)
    y_mat = np.einsum("xw,djsy->dxjswy", np.eye(x_piece), y_table.reshape(y_devices, j_local, y_devices, y_local))
    y_mat = y_mat.reshape(y_devices * group, y_devices, x_piece * y_local)
    seen = [[d ^ k if paired else k for k in range(y_devices)] for d in range(y_devices if paired else 1)]
    y_mats = np.stack([y_mat[:, owners].reshape(y_devices * group, -1) for owners in seen])
    mine = me if paired else 0
    x_mat = np.einsum("jk,ix->xjki", np.eye(j_local), x_table).reshape(x_extent * j_local, j_local * modes)
    syn, ana, x_mat = jnp.asarray(narrow(synth)), jnp.asarray(narrow(synth.T)), jnp.asarray(narrow(x_mat))
    y_mat = lax.dynamic_index_in_dim(jnp.asarray(narrow(y_mats)), mine, 0, keepdims=False)
    y_mat_t = lax.dynamic_index_in_dim(jnp.asarray(narrow(y_mats.swapaxes(1, 2))), mine, 0, keepdims=False)
    eye = jnp.eye(y_local, dtype=bf16)
    mix_up, mix_back = jnp.kron(point_weight.T, eye), jnp.kron(point_weight, eye)

    block_head = jax.ShapeDtypeStruct((x_piece, rows, lanes), bf16)
    full_field = jax.ShapeDtypeStruct(state_field.shape, bf16)
    held = pltpu.VMEM(block_head.shape, bf16)
    long, short = math.gcd(x_piece, 4), math.gcd(x_piece, 2)

    def plan(first, count, step):
        sub = x_piece // step
        where = lambda g, order: (0, 0, order[first + g // sub] * sub + g % sub, 0, 0)
        return sub, (count * sub,), pl.BlockSpec((steps, channels, step, y_local, depth), where)

    pairs = [(k, min(2, blocks - k)) for k in range(0, blocks, 2)]
    groups = [(1, 1)] + pairs[1:] + [(0, 1)] if blocks > 1 else pairs

    def head_call(first, count, after):
        sub, grid, field = plan(first, count, long)
        return call(
            functools.partial(head_body, sub), grid, [field, whole(ana.shape)],
            [whole(block_head.shape)] * count, [block_head] * count, (state_field, ana), order, [held], after=after,
        )

    def inner_call(first, count, middle, grads, after, carry):
        sub, grid, field = plan(first, count, short)
        tables = (mix_up, syn, ana)
        done = call(
            functools.partial(inner_body, sub, count), grid,
            [field] * 2 + [whole(arg.shape) for arg in tables] + [whole(block_head.shape)] * count + [ANY] * len(grads),
            [field] + [whole(block_head.shape)] * count, [full_field] + [block_head] * count,
            (state_field, cotangent, *tables, *middle[first : first + count], *grads), order,
            [held, held], {5 + count: 0} if grads else {}, after, carry,
        )
        return done[:1], done[1 : 1 + count], done[1 + count :]

    def outer_call(first, count, middle, grads, field, carry):
        sub, grid, spec = plan(first, count, long)
        tables = (mix_back, syn)
        done = call(
            functools.partial(outer_body, sub, count), grid,
            [spec] + [whole(arg.shape) for arg in tables] + [whole(block_head.shape)] * count + [ANY] * len(field),
            [spec], [full_field], (*grads, *tables, *middle[first : first + count], *field), order,
            [held], {3 + count: 0} if field else {}, (), carry,
        )
        return done[:1], done[1:]

    def small(body, outs, *args, after=()):
        shapes = [jax.ShapeDtypeStruct(out, bf16) for out in outs]
        return call(
            body, (1,), [whole(arg.shape) for arg in args], [whole(out) for out in outs], shapes, args, after=after
        )

    span = q_local * time_modes
    members = max(m for m in range(1, c_piece + 1) if c_piece % m == 0 and (m == 1 or m * span <= 128))
    packed = (x_devices, y_devices, c_piece // members, group, members * span)

    def exchange(pieces):
        shape = pieces.shape
        pieces = pieces.reshape((x_devices * y_devices,) + packed[2:])
        return lax.all_to_all(pieces, ("gx",) + YZ, 0, 0, tiled=True).reshape(shape)

    def send(k, piece):
        if not (paired and k):
            return piece
        return lax.ppermute(piece, YZ, [(d, d ^ k) for d in range(y_devices)])

    def settle(pieces, count, shape):
        if not paired:
            pieces = jnp.stack(pieces).reshape(y_devices, -1, lanes)
            pieces = lax.all_to_all(pieces, YZ, 0, 0, tiled=True).reshape((count,) + shape)
        return [pieces[k].reshape(shape) for k in range(count)]

    cells = (x_piece, c_piece, y_local, lanes)

    def analyze(heads):
        return small(y_down_body, [packed], y_mat, *settle(heads, y_devices, cells))[0]

    def mix(back, part, weight, after):
        part = exchange(part).reshape((x_devices, x_pieces, c_pieces) + packed[2:])
        kept, part = small(
            functools.partial(spectral_body, back), [(channels, span, j_local * modes), part.shape],
            part, x_mat, weight, after=after,
        )
        return kept, exchange(part).reshape(packed)

    def synthesize(part, after):
        pieces = small(y_up_body, [cells] * y_devices, part, y_mat_t, after=after)
        if paired:
            pieces = [piece.reshape(block_head.shape) for piece in pieces]
        late = pieces[6:] if paired else []
        return [send(k, piece) for k, piece in enumerate(pieces[: len(pieces) - len(late)])], late

    def rest(pieces, late):
        pieces = pieces + [send(len(pieces) + e, piece) for e, piece in enumerate(late)]
        return settle(pieces, blocks, block_head.shape)

    heads, after = [None] * blocks, ()
    for first, count in ((6, 2), (2, 4), (0, 2)) if blocks == 8 else ((0, blocks),):
        done = head_call(first, count, after)
        heads[first : first + count] = [send(first + e, piece) for e, piece in enumerate(done)]
        after = (done[0],) if first == 6 else tuple(heads[6:])
    part = analyze(heads)
    (weight,) = call(
        weight_body, (channels,),
        [pl.BlockSpec((j_local, q_local, 1, channels, time_modes, modes), lambda c: (0, 0, c, 0, 0, 0))],
        [pl.BlockSpec((1, channels, span, j_local * modes), lambda c: (c, 0, 0, 0))],
        [jax.ShapeDtypeStruct((channels, channels, span, j_local * modes), bf16)], (spectral_weight,), after=(part,),
    )
    modes_in, part = mix(False, part, weight, (mix_up, mix_back, y_mat_t))

    middle, late = synthesize(part, ())
    sent, grads = [(), ()], ()
    if not paired:
        middle = rest(middle, late)
    for first, count in groups:
        grads, done, late = inner_call(first, count, middle, grads, sent[-2], late)
        if late:
            middle, late = rest(middle, late), []
        heads[first : first + count] = [send(first + e, piece) for e, piece in enumerate(done)]
        sent.append(tuple(heads[max(first, 1) : first + count]) if paired else ())
    part = analyze(heads)
    grad_modes, part = mix(True, part, weight, ())
    spec = whole(modes_in.shape)
    (grad_spectral,) = call(
        outer_product_body, (j_local,), [spec, spec],
        [pl.BlockSpec((1,) + spectral_weight.shape[1:], lambda j: (j, 0, 0, 0, 0, 0))],
        [jax.ShapeDtypeStruct(spectral_weight.shape, jnp.float32)], (modes_in, grad_modes),
    )
    middle, late = synthesize(part, (grad_spectral,))
    if not paired:
        middle = rest(middle, late)
    field = ()
    for first, count in pairs:
        field, late = outer_call(first, count, middle, grads, field, late)
        if late:
            middle, late = rest(middle, late), []
    return field[0], grad_spectral


def solution(mesh):
    in_specs = (
        P("parts", None, "gx", YZ, None),
        P("parts", None, "gx", YZ, None),
        P(YZ, "gx", None, None, None, None),
        P(),
    )
    out_specs = (
        P("parts", None, "gx", YZ, None),
        P(("parts",) + YZ, "gx", None, None, None, None),
    )
    body = functools.partial(shards, mesh.shape["gx"], mesh.shape["gy"] * mesh.shape["gz"])
    return jax.shard_map(body, mesh=mesh, in_specs=in_specs, out_specs=out_specs, check_vma=False)
```

```python
import functools
import math

import jax
import jax.numpy as jnp
import ml_dtypes
import numpy as np
from jax import lax
from jax.experimental import pallas as pl
from jax.experimental.pallas import tpu as pltpu
from jax.sharding import PartitionSpec as P

YZ = ("gy", "gz")
HALF_ROOT = 1.0 / math.sqrt(2.0)
DENSITY = 1.0 / math.sqrt(2.0 * math.pi)


def basis(row_count, extent):
    row = np.arange(row_count)[:, None]
    cell = np.arange(extent)[None, :]
    radians = ((row + 1) // 2 * cell % extent) * (2.0 * math.pi / extent)
    wave = np.where(row % 2 == 0, np.cos(radians), np.sin(radians))
    scale = np.where(row == 0, math.sqrt(1.0 / extent), math.sqrt(2.0 / extent))
    return (wave * scale).astype(ml_dtypes.bfloat16).astype(np.float32)


def narrow(table):
    return np.asarray(table, dtype=ml_dtypes.bfloat16)


def dot(left, right, left_dim=1, right_dim=0):
    return lax.dot_general(
        left, right, (((left_dim,), (right_dim,)), ((), ())), preferred_element_type=jnp.float32
    )


def gelu_slope(value):
    size = jnp.abs(value)
    bell = jnp.exp2(value * value * (-0.5 * math.log2(math.e)))
    span = 1.0 + (0.3275911 * HALF_ROOT) * size
    t = pl.reciprocal(span, approx=True)
    t = t * (2.0 - span * t)
    tail = t * (
        0.5 * 0.254829592
        + t * (0.5 * -0.284496736 + t * (0.5 * 1.421413741 + t * (0.5 * -1.453152027 + t * (0.5 * 1.061405429))))
    )
    low = bell * (tail - DENSITY * size)
    return jnp.where(value >= 0.0, 1.0 - low, low)


ANY = pl.BlockSpec(memory_space=pl.ANY)


def call(body, grid, in_specs, out_specs, out_shape, args, order=None, scratch=(), aliases={}, after=(), carry=()):
    lead = 0 if order is None else 1
    count, outs = lead + len(args), len(out_shape)
    idle = len(after) + len(carry)

    def placed(*refs):
        ends = count + idle, count + idle + outs, count + idle + outs + len(carry)
        body(*refs[:count], *refs[ends[0] : ends[1]], *refs[ends[2] :])

    spec = pltpu.PrefetchScalarGridSpec(
        num_scalar_prefetch=lead,
        grid=grid,
        in_specs=list(in_specs) + [ANY] * idle,
        out_specs=list(out_specs) + [ANY] * len(carry),
        scratch_shapes=scratch,
    )
    kept = {count + len(after) + e: outs + e for e in range(len(carry))}
    return pl.pallas_call(
        placed,
        grid_spec=spec,
        out_shape=list(out_shape) + [jax.ShapeDtypeStruct(x.shape, x.dtype) for x in carry],
        input_output_aliases={lead + operand: out for operand, out in aliases.items()} | kept,
        compiler_params=pltpu.CompilerParams(vmem_limit_bytes=50 * 1024 * 1024),
        cost_estimate=pl.CostEstimate(flops=0, bytes_accessed=0, transcendentals=0),
    )(*(() if order is None else (order,)), *args, *after, *carry)


def whole(shape):
    return pl.BlockSpec(shape, lambda *_: (0,) * len(shape))


def wide(ref, cell, times):
    channels, _, y_local, depth = ref.shape[1:]
    return jnp.concatenate([ref[t, :, cell].reshape(channels * y_local, depth) for t in times], axis=1)


def admit(held, pieces, sub):
    for e, piece in enumerate(pieces):

        @pl.when(pl.program_id(0) == e * sub)
        def _(piece=piece):
            held[...] = piece[...]


def release(held, pieces, sub):
    for e, piece in enumerate(pieces):

        @pl.when(pl.program_id(0) == e * sub + sub - 1)
        def _(piece=piece):
            piece[...] = held[...]


def own_cells(sub, cells):
    return pl.ds(lax.rem(pl.program_id(0), sub) * cells, cells)


def head_body(sub, order_ref, field_ref, table_ref, *refs):
    heads, held = refs[:-1], refs[-1]
    steps, _, cells, _, depth = field_ref.shape
    first = lax.rem(pl.program_id(0), sub) * cells
    for cell in range(cells):
        total = 0.0
        for t in range(0, steps, 2):
            total += dot(wide(field_ref, cell, (t, t + 1)), table_ref[t * depth : (t + 2) * depth, :])
        held[first + cell] = total.astype(jnp.bfloat16)
    release(held, heads, sub)


def inner_body(sub, count, order_ref, field_ref, cot_ref, mix_ref, syn_ref, table_ref, *refs):
    mids, (grad_ref, *heads), (mid_held, head_held) = refs[:count], refs[-count - 3 : -2], refs[-2:]
    steps, channels, cells, y_local, depth = field_ref.shape
    rows = channels * y_local
    band = math.gcd(rows, 32)
    admit(mid_held, mids, sub)
    middle = mid_held[own_cells(sub, cells)].reshape(cells * rows, -1)
    total = 0.0
    for t in range(0, steps, 2):
        lanes = slice(t * depth, (t + 2) * depth)
        spread = dot(middle, syn_ref[:, lanes])
        bands = []
        for cell in range(cells):
            preact = spread[cell * rows : (cell + 1) * rows] + dot(mix_ref[...], wide(field_ref, cell, (t, t + 1)))
            cot = wide(cot_ref, cell, (t, t + 1))
            for r in range(0, rows, band):
                slope = gelu_slope(preact[r : r + band])
                bands.append(cot[r : r + band] * slope.astype(jnp.bfloat16))
        grad = jnp.concatenate(bands, axis=0)
        for cell in range(cells):
            for k in range(2):
                part = grad[cell * rows : (cell + 1) * rows, k * depth : (k + 1) * depth]
                grad_ref[t + k, :, cell] = part.reshape(channels, y_local, depth)
        total += dot(grad, table_ref[lanes, :])
    head_held[own_cells(sub, cells)] = total.astype(jnp.bfloat16).reshape((cells,) + head_held.shape[1:])
    release(head_held, heads, sub)


def outer_body(sub, count, order_ref, grad_ref, mix_ref, syn_ref, *refs):
    mids, out_ref, mid_held = refs[:count], refs[-2], refs[-1]
    steps, channels, cells, y_local, depth = grad_ref.shape
    rows = channels * y_local
    admit(mid_held, mids, sub)
    middle = mid_held[own_cells(sub, cells)].reshape(cells * rows, -1)
    for t in range(0, steps, 2):
        spread = dot(middle, syn_ref[:, t * depth : (t + 2) * depth])
        for cell in range(cells):
            total = spread[cell * rows : (cell + 1) * rows] + dot(mix_ref[...], wide(grad_ref, cell, (t, t + 1)))
            total = total.astype(jnp.bfloat16)
            for k in range(2):
                out_ref[t + k, :, cell] = total[:, k * depth : (k + 1) * depth].reshape(channels, y_local, depth)


def y_down_body(table_ref, *refs):
    pieces, out_ref = refs[:-1], refs[-1]
    cells, channels = pieces[0].shape[:2]
    planes, owners, groups, height, width = out_ref.shape
    members = channels // groups
    span = width // members
    for k in range(groups):
        done = []
        for c in range(k * members, (k + 1) * members):
            stacked = jnp.concatenate([piece[x, c] for piece in pieces for x in range(cells)], axis=0)
            done.append(dot(table_ref[...], stacked).astype(jnp.bfloat16))
        for g in range(planes):
            piece = jnp.concatenate([part[:, g * span : (g + 1) * span] for part in done], axis=1)
            out_ref[g, :, k] = piece.reshape(owners, height, width)


def y_up_body(rows_ref, table_ref, *pieces):
    planes, owners, groups, _, width = rows_ref.shape
    cells, channels, y_local, _ = pieces[0].shape
    members = channels // groups
    span = width // members
    for c in range(channels):
        lanes = slice(c % members * span, (c % members + 1) * span)
        stacked = jnp.concatenate(
            [
                jnp.concatenate([rows_ref[g, s, c // members][:, lanes] for g in range(planes)], axis=1)
                for s in range(owners)
            ],
            axis=0,
        )
        done = dot(table_ref[...], stacked).astype(jnp.bfloat16)
        for k, piece in enumerate(pieces):
            for x in range(cells):
                start = (k * cells + x) * y_local
                piece[x, c] = done[start : start + y_local]


def spectral_body(back, rows_ref, table_ref, weight_ref, modes_ref, out_ref):
    planes, x_pieces, c_pieces, groups, height, width = rows_ref.shape
    channels, span, lanes = modes_ref.shape
    members = width // span
    for h in range(c_pieces):
        for k in range(groups):
            stacked = jnp.concatenate(
                [rows_ref[g, x, h, k] for g in range(planes) for x in range(x_pieces)], axis=0
            )
            first = (h * groups + k) * members
            done = dot(stacked, table_ref[...], 0, 0).astype(jnp.bfloat16)
            modes_ref[first : first + members] = done.reshape(members, span, lanes)
    for h in range(c_pieces):
        for k in range(groups):
            mixed = []
            for m in range(members):
                to = (h * groups + k) * members + m
                total = 0.0
                for of in range(channels):
                    weight = weight_ref[to, of] if back else weight_ref[of, to]
                    total += weight.astype(jnp.float32) * modes_ref[of].astype(jnp.float32)
                mixed.append(total.astype(jnp.bfloat16))
            done = dot(table_ref[...], jnp.concatenate(mixed, axis=0), 1, 1).astype(jnp.bfloat16)
            for g in range(planes):
                for x in range(x_pieces):
                    start = (g * x_pieces + x) * height
                    out_ref[g, x, h, k] = done[start : start + height]


def weight_body(weight_ref, out_ref):
    j_local, q_local, _, channels = weight_ref.shape[:4]
    for o in range(channels):
        rows = [
            jnp.concatenate([weight_ref[j, q, 0, o].astype(jnp.float32) for j in range(j_local)], axis=1)
            for q in range(q_local)
        ]
        out_ref[0, o] = jnp.concatenate(rows, axis=0).astype(out_ref.dtype)


def outer_product_body(left_ref, right_ref, out_ref):
    _, q_local, channels, _, time_modes, modes = out_ref.shape
    for j in range(left_ref.shape[2] // modes):

        @pl.when(pl.program_id(0) == j)
        def _(j=j):
            lanes = slice(j * modes, (j + 1) * modes)
            left = left_ref[:, :, lanes].astype(jnp.float32)
            right = right_ref[:, :, lanes].astype(jnp.float32)
            for q in range(q_local):
                rows = slice(q * time_modes, (q + 1) * time_modes)
                for c in range(channels):
                    out_ref[0, q, c] = left[c, rows] * right[:, rows]


def shards(x_devices, y_devices, state_field, cotangent, spectral_weight, point_weight):
    steps, channels, x_local, y_local, depth = state_field.shape
    j_local, q_local = spectral_weight.shape[:2]
    time_modes, modes = spectral_weight.shape[4:]
    lanes = time_modes * modes
    rows = channels * y_local
    x_extent, y_extent = x_local * x_devices, y_local * y_devices
    bf16 = jnp.bfloat16

    x_pieces = math.gcd(x_local, y_devices)
    c_pieces = y_devices // x_pieces
    x_piece, c_piece = x_local // x_pieces, channels // c_pieces
    group = x_piece * j_local

    paired = c_pieces == 1 and y_devices & (y_devices - 1) == 0
    blocks = x_pieces
    me = lax.axis_index(YZ)
    order = jnp.arange(blocks, dtype=jnp.int32) ^ (me.astype(jnp.int32) if paired else 0)

    time_table, depth_table = basis(time_modes, steps), basis(modes, depth)
    x_table, y_table = basis(modes, x_extent), basis(modes, y_extent)
    synth = np.einsum("pt,qz->qptz", time_table, depth_table).reshape(lanes, steps * depth)
    y_mat = np.einsum("xw,djsy->dxjswy", np.eye(x_piece), y_table.reshape(y_devices, j_local, y_devices, y_local))
    y_mat = y_mat.reshape(y_devices * group, y_devices, x_piece * y_local)
    seen = [[d ^ k if paired else k for k in range(y_devices)] for d in range(y_devices if paired else 1)]
    y_mats = np.stack([y_mat[:, owners].reshape(y_devices * group, -1) for owners in seen])
    mine = me if paired else 0
    x_mat = np.einsum("jk,ix->xjki", np.eye(j_local), x_table).reshape(x_extent * j_local, j_local * modes)
    syn, ana, x_mat = jnp.asarray(narrow(synth)), jnp.asarray(narrow(synth.T)), jnp.asarray(narrow(x_mat))
    y_mat = lax.dynamic_index_in_dim(jnp.asarray(narrow(y_mats)), mine, 0, keepdims=False)
    y_mat_t = lax.dynamic_index_in_dim(jnp.asarray(narrow(y_mats.swapaxes(1, 2))), mine, 0, keepdims=False)
    eye = jnp.eye(y_local, dtype=bf16)
    mix_up, mix_back = jnp.kron(point_weight.T, eye), jnp.kron(point_weight, eye)

    block_head = jax.ShapeDtypeStruct((x_piece, rows, lanes), bf16)
    full_field = jax.ShapeDtypeStruct(state_field.shape, bf16)
    held = pltpu.VMEM(block_head.shape, bf16)
    long, short = math.gcd(x_piece, 4), math.gcd(x_piece, 2)

    def plan(first, count, step):
        sub = x_piece // step
        where = lambda g, order: (0, 0, order[first + g // sub] * sub + g % sub, 0, 0)
        return sub, (count * sub,), pl.BlockSpec((steps, channels, step, y_local, depth), where)

    pairs = [(k, min(2, blocks - k)) for k in range(0, blocks, 2)]
    groups = [(1, 1)] + pairs[1:] + [(0, 1)] if blocks > 1 else pairs

    def head_call(first, count, after):
        sub, grid, field = plan(first, count, long)
        return call(
            functools.partial(head_body, sub), grid, [field, whole(ana.shape)],
            [whole(block_head.shape)] * count, [block_head] * count, (state_field, ana), order, [held], after=after,
        )

    def inner_call(first, count, middle, grads, after, carry):
        sub, grid, field = plan(first, count, short)
        tables = (mix_up, syn, ana)
        done = call(
            functools.partial(inner_body, sub, count), grid,
            [field] * 2 + [whole(arg.shape) for arg in tables] + [whole(block_head.shape)] * count + [ANY] * len(grads),
            [field] + [whole(block_head.shape)] * count, [full_field] + [block_head] * count,
            (state_field, cotangent, *tables, *middle[first : first + count], *grads), order,
            [held, held], {5 + count: 0} if grads else {}, after, carry,
        )
        return done[:1], done[1 : 1 + count], done[1 + count :]

    def outer_call(first, count, middle, grads, field, carry):
        sub, grid, spec = plan(first, count, long)
        tables = (mix_back, syn)
        done = call(
            functools.partial(outer_body, sub, count), grid,
            [spec] + [whole(arg.shape) for arg in tables] + [whole(block_head.shape)] * count + [ANY] * len(field),
            [spec], [full_field], (*grads, *tables, *middle[first : first + count], *field), order,
            [held], {3 + count: 0} if field else {}, (), carry,
        )
        return done[:1], done[1:]

    def small(body, outs, *args, after=()):
        shapes = [jax.ShapeDtypeStruct(out, bf16) for out in outs]
        return call(
            body, (1,), [whole(arg.shape) for arg in args], [whole(out) for out in outs], shapes, args, after=after
        )

    span = q_local * time_modes
    members = max(m for m in range(1, c_piece + 1) if c_piece % m == 0 and (m == 1 or m * span <= 128))
    packed = (x_devices, y_devices, c_piece // members, group, members * span)

    def exchange(pieces):
        shape = pieces.shape
        pieces = pieces.reshape((x_devices * y_devices,) + packed[2:])
        return lax.all_to_all(pieces, ("gx",) + YZ, 0, 0, tiled=True).reshape(shape)

    def send(k, piece):
        if not (paired and k):
            return piece
        return lax.ppermute(piece, YZ, [(d, d ^ k) for d in range(y_devices)])

    def settle(pieces, count, shape):
        if not paired:
            pieces = jnp.stack(pieces).reshape(y_devices, -1, lanes)
            pieces = lax.all_to_all(pieces, YZ, 0, 0, tiled=True).reshape((count,) + shape)
        return [pieces[k].reshape(shape) for k in range(count)]

    cells = (x_piece, c_piece, y_local, lanes)

    def analyze(heads, after=()):
        return small(y_down_body, [packed], y_mat, *settle(heads, y_devices, cells), after=after)[0]

    def mix(back, part, weight):
        part = exchange(part).reshape((x_devices, x_pieces, c_pieces) + packed[2:])
        kept, part = small(
            functools.partial(spectral_body, back), [(channels, span, j_local * modes), part.shape],
            part, x_mat, weight,
        )
        return kept, exchange(part).reshape(packed)

    def synthesize(part, after):
        pieces = small(y_up_body, [cells] * y_devices, part, y_mat_t, after=after)
        if paired:
            pieces = [piece.reshape(block_head.shape) for piece in pieces]
        late = pieces[6:] if paired else []
        return [send(k, piece) for k, piece in enumerate(pieces[: len(pieces) - len(late)])], late

    def rest(pieces, late):
        pieces = pieces + [send(len(pieces) + e, piece) for e, piece in enumerate(late)]
        return settle(pieces, blocks, block_head.shape)

    heads, after = [None] * blocks, ()
    for first, count in ((6, 2), (2, 4), (0, 2)) if blocks == 8 else ((0, blocks),):
        done = head_call(first, count, after)
        heads[first : first + count] = [send(first + e, piece) for e, piece in enumerate(done)]
        after = (done[0],) if first == 6 else tuple(heads[6:])
    part = analyze(heads, (mix_up, mix_back, y_mat_t))
    (weight,) = call(
        weight_body, (channels,),
        [pl.BlockSpec((j_local, q_local, 1, channels, time_modes, modes), lambda c: (0, 0, c, 0, 0, 0))],
        [pl.BlockSpec((1, channels, span, j_local * modes), lambda c: (c, 0, 0, 0))],
        [jax.ShapeDtypeStruct((channels, channels, span, j_local * modes), bf16)], (spectral_weight,), after=(part,),
    )
    modes_in, part = mix(False, part, weight)

    middle, late = synthesize(part, ())
    sent, grads = [(), ()], ()
    if not paired:
        middle = rest(middle, late)
    for first, count in groups:
        grads, done, late = inner_call(first, count, middle, grads, sent[-2], late)
        if late:
            middle, late = rest(middle, late), []
        heads[first : first + count] = [send(first + e, piece) for e, piece in enumerate(done)]
        sent.append(tuple(heads[max(first, 1) : first + count]) if paired else ())
    part = analyze(heads)
    grad_modes, part = mix(True, part, weight)
    spec = whole(modes_in.shape)
    (grad_spectral,) = call(
        outer_product_body, (j_local,), [spec, spec],
        [pl.BlockSpec((1,) + spectral_weight.shape[1:], lambda j: (j, 0, 0, 0, 0, 0))],
        [jax.ShapeDtypeStruct(spectral_weight.shape, jnp.float32)], (modes_in, grad_modes),
    )
    middle, late = synthesize(part, (grad_spectral,))
    if not paired:
        middle = rest(middle, late)
    field = ()
    for first, count in pairs[:2] + [(4, blocks - 4)] if blocks > 4 else pairs:
        field, late = outer_call(first, count, middle, grads, field, late)
        if late:
            middle, late = rest(middle, late), []
    return field[0], grad_spectral


def solution(mesh):
    in_specs = (
        P("parts", None, "gx", YZ, None),
        P("parts", None, "gx", YZ, None),
        P(YZ, "gx", None, None, None, None),
        P(),
    )
    out_specs = (
        P("parts", None, "gx", YZ, None),
        P(("parts",) + YZ, "gx", None, None, None, None),
    )
    body = functools.partial(shards, mesh.shape["gx"], mesh.shape["gy"] * mesh.shape["gz"])
    return jax.shard_map(body, mesh=mesh, in_specs=in_specs, out_specs=out_specs, check_vma=False)
```
